32 devices in a mesh: fsdp: 8 (over z, x), ctx: 4 (over y, core).
Axes of the slice: x: 2, y: 2, z: 4, core: 2. Of those that a mesh axis runs over, the one named last changes fastest.
Arguments:
- hidden_in: bfloat16 [8, 1536, 768], P('fsdp', 'ctx'), may hold values from -6 to 6
- segment_ids: int32 [8, 1536], P('fsdp', 'ctx'), may hold values from 0 to 2, as said below
- positions: int32 [8, 1536], P('fsdp', 'ctx'), may hold values from 0 to 2556, as said below
- norm1_gain: bfloat16 [768], P('fsdp'), may hold values from 0.5 to 1.5
- qkv_weight: bfloat16 [768, 2304], P('fsdp'), may hold values from -0.21875 to 0.21875
- out_weight: bfloat16 [768, 768], P('fsdp'), may hold values from -6 to 6
- norm2_gain: bfloat16 [768], P('fsdp'), may hold values from 0.5 to 1.5
- in_weight: bfloat16 [768, 2304], P('fsdp'), may hold values from -0.21875 to 0.21875
- down_weight: bfloat16 [1152, 768], P('fsdp'), may hold values from -0.375 to 0.375
- out_cot: bfloat16 [8, 1536, 768], P('fsdp', 'ctx'), may hold values from -6 to 6
Outputs:
- out: bfloat16 [8, 1536, 768], P('fsdp', 'ctx')
- in_grad: float32 [8, 1536, 768], P('fsdp', 'ctx')
- norm1_gain_grad: float32 [768], P('fsdp')
- qkv_weight_grad: float32 [768, 2304], P('fsdp')
- out_weight_grad: float32 [768, 768], P('fsdp')
- norm2_gain_grad: float32 [768], P('fsdp')
- in_weight_grad: float32 [768, 2304], P('fsdp')
- down_weight_grad: float32 [1152, 768], P('fsdp')
The draws below stay inside these ranges and needn't reach their ends.
Inputs may be any that keep to these rules, and one draw needn't show every extreme that they name: `segment_ids`: in each sequence the ids never fall: 0 on its first tokens, 1 from a place within the first 384 tokens to a place within the last 384, 2 on the tokens after it. Within a document the positions rise by one from token to token; the first document of each sequence starts at 0, the second ends at 2556, the third starts at some value below 1024.
All inputs are finite; a program needn't handle non-finite values.
Results may differ from the reference program's by a relative error of at most 0.015.
Values may be sent and summed in bfloat16 or wider, within the bound.
No kernel may reach another device: no remote copies, remote signals or barrier semaphores. Data moves between devices by JAX's collectives and lax.ppermute only.
A program may use at most 256 MiB of HBM per device.

```python
import jax
import jax.numpy as jnp
from jax import lax

D = 768
HEADS = 12
HEAD_DIM = 64
FF = 1152
TOK_DEV = 384
LENGTH = 1536
SEQS = 8


def boundaries(key):
    head_len = jax.random.randint(jax.random.fold_in(key, 11), (SEQS, 1), 1, TOK_DEV)
    tail_len = jax.random.randint(jax.random.fold_in(key, 12), (SEQS, 1), 1, TOK_DEV)
    indices = jnp.arange(LENGTH, dtype=jnp.int32)[None, :]
    doc_ids = (indices >= head_len).astype(jnp.int32) + (indices >= LENGTH - tail_len).astype(jnp.int32)
    return (head_len, tail_len, indices, doc_ids)


def draw_segment_ids(key, part):
    shared = boundaries(key)
    return shared[3]


def draw_positions(key, part):
    head_len, tail_len, indices, doc_ids = boundaries(key)
    key = jax.random.fold_in(key, 2)
    third_offset = jax.random.randint(key, (SEQS, 1), 0, 1024)
    middle_offset = 1021 + head_len + tail_len
    offsets = jnp.concatenate([jnp.zeros_like(head_len), middle_offset, third_offset], axis=1)
    starts = jnp.concatenate([jnp.zeros_like(head_len), head_len, LENGTH - tail_len], axis=1)
    picked_offsets = jnp.take_along_axis(offsets, doc_ids, axis=1)
    picked_starts = jnp.take_along_axis(starts, doc_ids, axis=1)
    return (picked_offsets + indices - picked_starts).astype(jnp.int32)


def level_of(rng, shape, pieces, least, top_value):
    level = 1.0
    for position, parts in pieces:
        draws = jax.random.uniform(jax.random.fold_in(jax.random.fold_in(rng, 6), position), (parts,), jnp.float32, least / len(pieces), top_value / len(pieces))
        level = level * jnp.repeat(jnp.exp(draws), shape[position] // parts).reshape((-1,) + (1,) * (len(shape) - 1 - position))
    return level


def bell_draw(stream_key, dims, deviation, most, split=(), kind=jnp.bfloat16):
    loudness = level_of(stream_key, dims, split, -0.22, 0.18) if split else 1.0
    array = jax.random.normal(stream_key, dims, jnp.float32) * deviation * loudness
    return jnp.minimum(jnp.maximum(array, -most), most).astype(kind)


def setup_inputs(seed: int = 0) -> dict:
    key_list = jax.random.split(jax.random.key(seed), 11)
    return {
        "hidden_in": bell_draw(key_list[0], (SEQS, LENGTH, D), 1.0, 6.0, ((0, 8), (1, 4))),
        "segment_ids": draw_segment_ids(jax.random.fold_in(key_list[10], 71), 0),
        "positions": draw_positions(jax.random.fold_in(key_list[10], 71), 0),
        "norm1_gain": jnp.clip(1.0 + 0.1 * jax.random.normal(key_list[3], (D,), jnp.float32), 0.5, 1.5).astype(jnp.bfloat16),
        "qkv_weight": bell_draw(key_list[4], (D, 3 * D), D ** -0.5, 0.21875, ((0, 8),)),
        "out_weight": bell_draw(key_list[5], (D, D), (max(1, 3 * D // LENGTH)) ** -0.5, 6.0, ((0, 8),)),
        "norm2_gain": jnp.clip(1.0 + 0.1 * jax.random.normal(key_list[6], (D,), jnp.float32), 0.5, 1.5).astype(jnp.bfloat16),
        "in_weight": bell_draw(key_list[7], (D, 2 * FF), D ** -0.5, 0.21875, ((0, 8),)),
        "down_weight": bell_draw(key_list[8], (FF, D), (FF // 4) ** -0.5, 0.375, ((0, 8),)),
        "out_cot": bell_draw(key_list[9], (SEQS, LENGTH, D), 1.0, 6.0, ((0, 8), (1, 4))),
    }


rope_base = 160000.0
norm_eps = 1e-05
masked_score = -1e+30
highest = lax.Precision.HIGHEST

@jax.custom_vjp
def low(v):
    return lax.optimization_barrier(v.astype(jnp.bfloat16)).astype(jnp.float32)

@jax.custom_vjp
def low_back(v):
    return v

def low_keep(v):
    return (low(v), None)

def low_pass(kept, grad):
    return (grad,)

def back_keep(v):
    return (v, None)

def back_low(kept, grad):
    return (low(grad),)
low.defvjp(low_keep, low_pass)
low_back.defvjp(back_keep, back_low)

def matmul(left, right):
    return jnp.dot(left, right, precision=highest)

def normalize(fields):
    row_mean = lax.optimization_barrier(jnp.mean(fields, axis=-1, keepdims=True))
    centred = fields - row_mean
    variance = lax.optimization_barrier(jnp.mean(centred * centred, axis=-1, keepdims=True))
    return centred * lax.rsqrt(variance + norm_eps)

def rope_tables(places):
    half_dim = HEAD_DIM // 2
    frequency = rope_base ** (-2.0 * jnp.arange(half_dim, dtype=jnp.float32) / HEAD_DIM)
    angles = places.astype(jnp.float32)[:, None] * frequency[None, :]
    return (jnp.cos(angles)[:, None, :], jnp.sin(angles)[:, None, :])

def rotate(fields, cosine_table, sine_table):
    half_dim = HEAD_DIM // 2
    lower_half = fields[..., :half_dim]
    upper_half = fields[..., half_dim:]
    return jnp.concatenate([lower_half * cosine_table - upper_half * sine_table, upper_half * cosine_table + lower_half * sine_table], axis=-1)

def project(fields, params, places):
    gain_one, w_qkv = (params[0], params[1])
    model_width = fields.shape[-1]
    length_all = fields.shape[0]
    h_one = low(normalize(fields) * gain_one)
    qkv_proj = low_back(matmul(h_one, w_qkv))
    cosine_table, sine_table = rope_tables(places)
    query_low = low(rotate(qkv_proj[:, :model_width].reshape(length_all, HEADS, HEAD_DIM), cosine_table, sine_table))
    key_low = low(rotate(qkv_proj[:, model_width:2 * model_width].reshape(length_all, HEADS, HEAD_DIM), cosine_table, sine_table))
    value_low = low(qkv_proj[:, 2 * model_width:].reshape(length_all, HEADS, HEAD_DIM))
    return (query_low, key_low, value_low)

def own_maxima(query_low, key_low, doc_ids):
    length_all = query_low.shape[0]
    blocks = length_all // TOK_DEV
    score_scale = HEAD_DIM ** (-0.5)
    query_blocks = query_low.reshape(blocks, TOK_DEV, HEADS, HEAD_DIM)
    key_blocks = key_low.reshape(blocks, TOK_DEV, HEADS, HEAD_DIM)
    doc_blocks = doc_ids.reshape(blocks, TOK_DEV)

    def one_block(inputs):
        query_rows, key_rows, doc_rows = inputs
        scores = jnp.einsum('qhe,khe->qhk', query_rows, key_rows, precision=highest) * score_scale
        scores = jnp.where((doc_rows[:, None] == doc_rows[None, :])[:, None, :], scores, masked_score)
        return lax.optimization_barrier(jnp.max(scores, axis=-1))
    return lax.map(one_block, (query_blocks, key_blocks, doc_blocks)).reshape(length_all, HEADS)

def attention(query_low, key_low, value_low, doc_ids, shift):
    length_all = query_low.shape[0]
    block_rows = min(512, length_all)
    score_scale = HEAD_DIM ** (-0.5)
    query_blocks = query_low.reshape(length_all // block_rows, block_rows, HEADS, HEAD_DIM)
    doc_blocks = doc_ids.reshape(length_all // block_rows, block_rows)
    shift_blocks = shift.reshape(length_all // block_rows, block_rows, HEADS)

    def one_block(inputs):
        query_rows, doc_rows, shift_rows = inputs
        scores = jnp.einsum('qhe,khe->hqk', query_rows, key_low, precision=highest) * score_scale
        scores = jnp.where(doc_rows[None, :, None] == doc_ids[None, None, :], scores, masked_score)
        scores = low_back(scores)
        expo_f = jnp.exp(scores - shift_rows.T[:, :, None])
        total = lax.optimization_barrier(jnp.sum(expo_f, axis=-1))
        acc = jnp.einsum('hqk,khe->qhe', low(expo_f), value_low, precision=highest)
        return low_back(acc) / total.T[:, :, None]
    mixed_f = lax.map(jax.checkpoint(one_block), (query_blocks, doc_blocks, shift_blocks))
    return mixed_f.reshape(length_all, HEADS * HEAD_DIM)

def forward(fields, params, doc_ids, places, shift):
    gain_one, w_qkv, w_out, gain_two, w_in, w_down = params
    query_low, key_low, value_low = project(fields, params, places)
    mixed_f = attention(query_low, key_low, value_low, doc_ids, shift)
    mixed_low = low(mixed_f)
    resid = fields + low_back(matmul(mixed_low, w_out))
    h_two = low(normalize(resid) * gain_two)
    up_all = low_back(matmul(h_two, w_in))
    ff_width = w_down.shape[0]
    mid_low = low(jax.nn.gelu(up_all[:, :ff_width], approximate=False) * up_all[:, ff_width:])
    return resid + low_back(matmul(mid_low, w_down))

def reference(hidden_in, segment_ids, positions, norm1_gain, qkv_weight, out_weight, norm2_gain, in_weight, down_weight, out_cot):
    params = tuple((member.astype(jnp.float32) for member in (norm1_gain, qkv_weight, out_weight, norm2_gain, in_weight, down_weight)))

    def one_sequence(totals, inputs):
        fields, doc_ids, places, cotangent = inputs
        fields_f = fields.astype(jnp.float32)
        query_low, key_low, value_low = project(fields_f, params, places)
        shift = own_maxima(query_low, key_low, doc_ids)

        def run(fields_in, weight_list):
            return forward(fields_in, weight_list, doc_ids, places, shift)
        output, pullback = jax.vjp(run, fields_f, params)
        grad_fields, grad_params = pullback(cotangent.astype(jnp.float32))
        totals = tuple((total + member for total, member in zip(totals, grad_params)))
        return (totals, (output.astype(jnp.bfloat16), grad_fields))
    zeros = tuple((jnp.zeros(member.shape, jnp.float32) for member in params))
    totals, (outputs, in_grads) = lax.scan(one_sequence, zeros, (hidden_in, segment_ids, positions, out_cot))
    return (outputs, in_grads, totals[0], totals[1], totals[2], totals[3], totals[4], totals[5])
```

```python
import functools
import math

import jax
import jax.numpy as jnp
from jax import lax
from jax.experimental import pallas as pl
from jax.experimental.pallas import tpu as pltpu
from jax.sharding import PartitionSpec as P

HEAD_DIM = 64
rope_base = 160000.0
norm_eps = 1e-05
BF = jnp.bfloat16
F32 = jnp.float32
AXES = ("fsdp", "ctx")
EXP_SCALE = HEAD_DIM ** (-0.5) * math.log2(math.e)
MIB = 2**20


def nt(a, b):
    return lax.dot_general(a, b, (((1,), (1,)), ((), ())), preferred_element_type=F32)


def nn(a, b):
    return lax.dot_general(a, b, (((1,), (0,)), ((), ())), preferred_element_type=F32)


def tn(a, b):
    return lax.dot_general(a, b, (((0,), (0,)), ((), ())), preferred_element_type=F32)


def lanes(shape):
    return lax.broadcasted_iota(jnp.int32, shape, 1)


def split3(v):
    hi = v.astype(BF).astype(F32)
    rest = v - hi
    mid = rest.astype(BF).astype(F32)
    low = (rest - mid).astype(BF).astype(F32)
    return hi, mid, low


def swap_halves(u, lane):
    width = u.shape[1]
    return jnp.where((lane % 64) < 32, pltpu.roll(u, width - 32, 1), pltpu.roll(u, 32, 1))


def permute(x, fn, F, C):
    return lax.ppermute(x, AXES, [(i, fn(i)) for i in range(F * C)])


def flip_ctx(x, bit, F, C):
    return permute(x, lambda i: (i // C) * C + ((i % C) ^ bit), F, C)


def flip_fsdp(x, F, C):
    return permute(x, lambda i: (((i // C) ^ 1) * C) + i % C, F, C)


def ring(x, F, C):
    return permute(x, lambda i: (i + 2 * C) % (F * C), F, C)


def ctx_bits(C):
    bits = []
    b = C // 2
    while b:
        bits.append(b)
        b //= 2
    return bits


def gather_ctx(x, F, C):
    have = x[None]
    order = [0]
    for b in ctx_bits(C):
        have = jnp.concatenate([have, flip_ctx(have, b, F, C)], axis=0)
        order = order + [p ^ b for p in order]
    return have, order


def reduce_ctx(parts, F, C):
    for b in reversed(ctx_bits(C)):
        half = parts.shape[0] // 2
        got = flip_ctx(parts[half:].astype(BF), b, F, C)
        parts = parts[:half] + got.astype(F32)
    return parts[0]


def reduce_steps(grads, F, C):
    core = lax.axis_index("ctx") % 2
    keep_parts, give_parts = [], []
    for g in grads:
        g3 = g.astype(BF).reshape(F, g.shape[0] // F, g.shape[1])
        half = g.shape[1] // 2
        for j in range(0, half, 384):
            a = g3[:, :, j : j + 384]
            b = g3[:, :, half + j : half + j + 384]
            keep_parts.append(jnp.where(core == 0, a, b))
            give_parts.append(jnp.where(core == 0, b, a))
    give = jnp.concatenate(give_parts, axis=1)
    keep = jnp.concatenate(keep_parts, axis=1)
    yield give
    got = flip_ctx(give, 1, F, C)
    acc = (keep.astype(F32) + got.astype(F32)).astype(BF)
    yield acc
    Z = F // 2
    me = lax.axis_index("fsdp")
    z, xx = me // 2, me % 2
    total = None
    for s in range(Z):
        d = lax.rem(z - 1 - s + Z, Z)
        got = flip_fsdp(lax.dynamic_index_in_dim(acc, d * 2 + 1 - xx, 0, False), F, C)
        mine = lax.dynamic_index_in_dim(acc, d * 2 + xx, 0, False).astype(F32) + got.astype(F32)
        total = mine if total is None else mine + arrived.astype(F32)
        if s < Z - 1:
            send = total.astype(BF)
            yield send
            arrived = ring(send, F, C)
    for b in ctx_bits(C)[:-1]:
        total = total + flip_ctx(total.astype(BF), b, F, C).astype(F32)
    other = flip_ctx(total.astype(BF), 1, F, C).astype(F32)
    first = jnp.where(core == 0, total, other)
    second = jnp.where(core == 0, other, total)
    outs = []
    row = 0
    for g in grads:
        n, count = g.shape[0] // F, g.shape[1] // 768
        cols = [side[row + j * n : row + (j + 1) * n] for side in (first, second) for j in range(count)]
        row += n * count
        outs.append(jnp.concatenate(cols, axis=1))
    yield outs


def finish(steps):
    for last in steps:
        pass
    return last


def unpack_kernel(idx_ref, own_ref, got_ref, *refs, F, places):
    outs, sems = refs[:-1], refs[-1]
    piece = own_ref.shape[0] // F
    copies = []
    for j in range(F):
        for side, src in ((0, own_ref), (1, got_ref)):
            for row, n, o, half, col in places:
                r = pl.multiple_of(idx_ref[j] * n, n)
                c = pl.multiple_of(idx_ref[F + side] * half + col, 128)
                copies.append(
                    pltpu.make_async_copy(
                        src.at[pl.ds(j * piece + row, n), :],
                        outs[o].at[pl.ds(r, n), pl.ds(c, src.shape[1])],
                        sems.at[len(copies)],
                    )
                )
    for c in copies:
        c.start()
    for c in copies:
        c.wait()


def unpack(own, got, idx, F, places, shapes):
    return pl.pallas_call(
        functools.partial(unpack_kernel, F=F, places=places),
        in_specs=[
            pl.BlockSpec(memory_space=pltpu.SMEM),
            pl.BlockSpec(memory_space=pl.ANY),
            pl.BlockSpec(memory_space=pl.ANY),
        ],
        out_specs=[pl.BlockSpec(memory_space=pltpu.VMEM)] * len(shapes),
        out_shape=[jax.ShapeDtypeStruct(s, own.dtype) for s in shapes],
        scratch_shapes=[pltpu.SemaphoreType.DMA((2 * F * len(places),))],
        compiler_params=pltpu.CompilerParams(vmem_limit_bytes=32 * MIB),
        name="unpack",
    )(idx, own, got)


def project_kernel(idx_ref, x_ref, gain_ref, own_ref, got_ref, cos_ref, sin_ref, h_ref, q_ref, k_ref, v_ref, w_ref, sems, *, F, n):
    rows, width = h_ref.shape
    half = w_ref.shape[1] // 2
    piece = own_ref.shape[0] // F

    def copies():
        made = []
        for j in range(F):
            for side, src in ((0, own_ref), (1, got_ref)):
                r = pl.multiple_of(idx_ref[j] * n, n)
                c = pl.multiple_of(idx_ref[F + side] * half, 128)
                made.append(
                    pltpu.make_async_copy(
                        src.at[pl.ds(j * piece, n), :], w_ref.at[pl.ds(r, n), pl.ds(c, half)], sems.at[len(made)]
                    )
                )
        return made

    @pl.when(pl.program_id(0) == 0)
    def _():
        made = copies()
        for c in made:
            c.start()
        for c in made:
            c.wait()

    x = x_ref[0, :rows, :].astype(F32)
    centred = x - jnp.mean(x, axis=1, keepdims=True)
    var = jnp.mean(centred * centred, axis=1, keepdims=True)
    h = (centred * lax.rsqrt(var + norm_eps) * gain_ref[...]).astype(BF)
    h_ref[...] = h
    cos, sin = cos_ref[...], sin_ref[...]
    lane = lanes((rows, 128))

    def rope_into(ref, offset):
        for j in range(0, width, 256):
            u = nn(h, w_ref[:, offset + j : offset + j + 256])
            for i in (0, 128):
                t = u[:, i : i + 128]
                ref[:, j + i : j + i + 128] = (t * cos + swap_halves(t, lane) * sin).astype(BF)

    rope_into(k_ref, width)
    for j in range(0, width, 256):
        v_ref[:, j : j + 256] = nn(h, w_ref[:, 2 * width + j : 2 * width + j + 256]).astype(BF)

    @pl.when(pl.program_id(0) == 0)
    def _():
        rope_into(q_ref, 0)


def project(xs, gain, own, got, idx, cos, sin, rows, F):
    C, _, width = xs.shape
    blk = pl.BlockSpec((rows, width), lambda i: (i, 0))
    tab = pl.BlockSpec((rows, 128), lambda i: (i, 0))
    whole = lambda i: (0, 0)
    out = jax.ShapeDtypeStruct((C * rows, width), BF)
    return pl.pallas_call(
        functools.partial(project_kernel, F=F, n=width // F),
        grid=(C,),
        in_specs=[
            pl.BlockSpec(memory_space=pltpu.SMEM),
            pl.BlockSpec((1,) + xs.shape[1:], lambda i: (i, 0, 0)),
            pl.BlockSpec((1, width), whole),
            pl.BlockSpec(memory_space=pl.ANY),
            pl.BlockSpec(memory_space=pl.ANY),
            tab,
            tab,
        ],
        out_specs=[blk, pl.BlockSpec((rows, width), whole), blk, blk, pl.BlockSpec((width, 3 * width), whole)],
        out_shape=[out, jax.ShapeDtypeStruct((rows, width), BF), out, out, jax.ShapeDtypeStruct((width, 3 * width), BF)],
        scratch_shapes=[pltpu.SemaphoreType.DMA((2 * F,))],
        compiler_params=pltpu.CompilerParams(vmem_limit_bytes=40 * MIB),
        name="project",
    )(idx, xs, gain, own, got, cos, sin)


def forward_kernel(q_ref, k_ref, v_ref, f_ref, fq_ref, after_ref, mix_ref, low_ref, m_ref, t_ref, *, rows, blocks):
    low = lanes((rows, 128)) < 64
    q, fq = q_ref[...], fq_ref[...]
    outs = []
    for x in range(2):
        pick = low if x == 0 else ~low
        qx = jnp.where(pick, q, fq)
        acc = None
        for j in range(blocks):
            sl = pl.ds(j * rows, rows)
            f = f_ref[sl, :]
            kx = jnp.where(pick, k_ref[sl, :], f)
            vx = jnp.where(pick, v_ref[sl, :], f)
            s = nt(qx, kx)
            if j == 0:
                top = jnp.max(s, axis=1, keepdims=True)
            p = jnp.exp2((s - top) * EXP_SCALE).astype(BF)
            a = nn(p, vx)
            acc = a if acc is None else acc + a
        at = 70 if x == 0 else 6
        tot = acc[:, at : at + 1]
        outs.append((acc / tot, top, tot))
    (a0, m0, t0), (a1, m1, t1) = outs
    mix = jnp.where(low, a0, a1)
    mix_ref[...] = mix
    low_ref[...] = mix.astype(BF)
    m_ref[...] = jnp.where(low, m1, m0)
    t_ref[...] = jnp.where(low, t0, t1)


def attend(q, k, v, f, fq, after, first, n):
    rows, T = q.shape[0], k.shape[0]
    qs = pl.BlockSpec((rows, 128), lambda i: (0, i + first))
    ks = pl.BlockSpec((T, 128), lambda i: (0, i + first))
    cf = pl.BlockSpec((T, 128), lambda i: (0, 0))
    cq = pl.BlockSpec((rows, 128), lambda i: (0, 0))
    oq = pl.BlockSpec((rows, 128), lambda i: (0, i))
    out = jax.ShapeDtypeStruct((rows, 128 * n), F32)
    return pl.pallas_call(
        functools.partial(forward_kernel, rows=rows, blocks=T // rows),
        grid=(n,),
        in_specs=[qs, ks, ks, cf, cq, pl.BlockSpec(memory_space=pl.ANY)],
        out_specs=[oq] * 4,
        out_shape=[out, jax.ShapeDtypeStruct((rows, 128 * n), BF), out, out],
        compiler_params=pltpu.CompilerParams(vmem_limit_bytes=40 * MIB),
        name="attend",
    )(q, k, v, f, fq, after)


def backward_kernel(
    q_ref, k_ref, v_ref, f_ref, fq_ref, m_ref, t_ref, mix_ref, gm_ref, cos_ref, sin_ref, after_ref,
    dq_ref, dk_ref, dv_ref, sk_ref, sv_ref, *, rows, blocks,
):
    lane = lanes((rows, 128))
    low = lane < 64
    slot = lane % 64
    q = q_ref[...]
    ga = gm_ref[...] / t_ref[...]
    prod = ga * mix_ref[...]
    hi, mid, lo = split3(m_ref[...])
    fq = jnp.where(slot == 3, -hi, jnp.where(slot == 4, -mid, jnp.where(slot == 5, -lo, fq_ref[...].astype(F32)))).astype(BF)
    gab = ga.astype(BF)
    dqs = []
    for x in range(2):
        pick = low if x == 0 else ~low
        qx = jnp.where(pick, q, fq)
        delta = jnp.sum(jnp.where(pick, prod, 0.0), axis=1, keepdims=True)
        h3, m3, l3 = split3(jnp.broadcast_to(delta, (rows, 128)))
        gf = jnp.where(slot == 6, -h3, jnp.where(slot == 7, -m3, jnp.where(slot == 8, -l3, 0.0))).astype(BF)
        gx = jnp.where(pick, gab, gf)
        gxt = gx.T[64 * x : 64 * x + 64]
        qxt = qx.T[64 * x : 64 * x + 64]
        dq = None
        for j in range(blocks):
            sl = pl.ds(j * rows, rows)
            f = f_ref[sl, :]
            kx = jnp.where(pick, k_ref[sl, :], f)
            vx = jnp.where(pick, v_ref[sl, :], f)
            p = jnp.exp2(nt(qx, kx) * EXP_SCALE)
            ds = (p * nt(gx, vx)).astype(BF)
            d = nn(ds, kx)
            dq = d if dq is None else dq + d
            sv_ref[64 * x : 64 * x + 64, sl] = nn(gxt, p.astype(BF))
            sk_ref[64 * x : 64 * x + 64, sl] = nn(qxt, ds)
        dqs.append(dq)
    scale = HEAD_DIM ** (-0.5)

    def unrope(u, sl):
        return (u * cos_ref[sl, :] - swap_halves(u, lane) * sin_ref[sl, :]).astype(BF)

    dq_ref[...] = unrope(jnp.where(low, dqs[0], dqs[1]) * scale, pl.ds(0, rows))
    for j in range(blocks):
        sl = pl.ds(j * rows, rows)
        dv_ref[sl, :] = sv_ref[:, sl].T.astype(BF)
        dk_ref[sl, :] = unrope(sk_ref[:, sl].T * scale, sl)


def attend_back(q, k, v, f, fq, top, tot, mix, gm, cos, sin, after, first, n):
    rows, T = q.shape[0], k.shape[0]
    qs = pl.BlockSpec((rows, 128), lambda i: (0, i + first))
    ks = pl.BlockSpec((T, 128), lambda i: (0, i + first))
    cf = pl.BlockSpec((T, 128), lambda i: (0, 0))
    cq = pl.BlockSpec((rows, 128), lambda i: (0, 0))
    oq = pl.BlockSpec((rows, 128), lambda i: (0, i))
    ok = pl.BlockSpec((T, 128), lambda i: (0, i))
    return pl.pallas_call(
        functools.partial(backward_kernel, rows=rows, blocks=T // rows),
        grid=(n,),
        in_specs=[qs, ks, ks, cf, cq, oq, oq, oq, qs, cf, cf, pl.BlockSpec(memory_space=pl.ANY)],
        out_specs=[oq, ok, ok],
        out_shape=[jax.ShapeDtypeStruct((rows, 128 * n), BF)] + [jax.ShapeDtypeStruct((T, 128 * n), BF)] * 2,
        scratch_shapes=[pltpu.VMEM((128, T), F32), pltpu.VMEM((128, T), F32)],
        compiler_params=pltpu.CompilerParams(vmem_limit_bytes=48 * MIB),
        name="attend_back",
    )(q, k, v, f, fq, top, tot, mix, gm, cos, sin, after)


def normalize(fields):
    centred = fields - jnp.mean(fields, axis=-1, keepdims=True)
    variance = jnp.mean(centred * centred, axis=-1, keepdims=True)
    inv_root = lax.rsqrt(variance + norm_eps)
    return centred * inv_root, inv_root


def norm_back(grad_out, normed, inv_root, gain):
    scaled = grad_out * gain
    return inv_root * (
        scaled
        - jnp.mean(scaled, axis=-1, keepdims=True)
        - normed * jnp.mean(scaled * normed, axis=-1, keepdims=True)
    )


def tables(docs, places):
    lane = jnp.arange(128)
    frequency = rope_base ** (-2.0 * (lane % 32).astype(F32) / HEAD_DIM)
    angles = places.astype(F32)[:, None] * frequency[None, :]
    sign = jnp.where(lane % 64 < 32, -1.0, 1.0)
    slot = lane % 64
    same = (docs[:, None] == slot[None, :]) & (slot < 3)[None, :]
    ones = ((slot >= 3) & (slot < 9))[None, :]
    feats = jnp.where(same | ones, 1.0, 0.0).astype(BF)
    return jnp.cos(angles), jnp.sin(angles) * sign, feats


def core_half(shard, core):
    half = shard.shape[1] // 2
    return lax.dynamic_slice_in_dim(shard, core * half, half, 1)


def gather_steps(piece, F, C):
    Z = F // 2
    same = piece
    for k in range(Z):
        other = flip_fsdp(same, F, C)
        nxt = ring(same, F, C) if k < Z - 1 else None
        yield same, other
        same = nxt


def owners_of(F):
    Z = F // 2
    me = lax.axis_index("fsdp")
    z, xx = me // 2, me % 2
    owners = []
    for k in range(Z):
        base = lax.rem(z - k + Z, Z) * 2
        owners += [base + xx, base + 1 - xx]
    return owners


def both_cores(pieces, F, C):
    own = jnp.concatenate(pieces, axis=0)
    return own, flip_ctx(own, 1, F, C)


def body(
    F, C, hidden_in, segment_ids, positions, norm1_gain, qkv_weight, out_weight, norm2_gain, in_weight, down_weight, out_cot
):
    width = hidden_in.shape[-1]
    rows = hidden_in.shape[1]
    inputs = hidden_in.reshape(rows, width)
    docs = segment_ids.reshape(-1)
    places = positions.reshape(-1)
    extra = jnp.zeros((16, width), BF)
    meta = jnp.stack([docs, places // 256, places % 256]).astype(BF)
    extra = lax.dynamic_update_slice(extra, meta, (0, 0))
    xs, _ = gather_ctx(jnp.concatenate([inputs, extra], axis=0), F, C)
    core = lax.axis_index("ctx") % 2
    owners = owners_of(F)
    idx = jnp.stack([jnp.asarray(o, jnp.int32) for o in owners] + [core, 1 - core]).astype(jnp.int32)
    n = width // F
    half = core_half(qkv_weight, core)
    gain_rows = lax.dynamic_update_slice(
        jnp.zeros((16, half.shape[1]), BF), jnp.concatenate([norm1_gain, norm2_gain])[None], (0, 0)
    )
    pieces = [p for step in gather_steps(jnp.concatenate([half, gain_rows], axis=0), F, C) for p in step]
    own_a, got_a = both_cores(pieces, F, C)
    gain_pieces = own_a.reshape(F, n + 16, -1)[:, n, : 2 * n].astype(F32)
    place = jnp.stack(owners)[None, :] == jnp.arange(F)[:, None]
    gains = jnp.sum(jnp.where(place[:, :, None], gain_pieces[None], 0.0), axis=1).reshape(F, 2, n)
    gain_one, gain_two = gains[:, 0].reshape(1, width), gains[:, 1].reshape(1, width)

    all_meta = xs[:, rows : rows + 3, :rows].astype(jnp.int32)
    all_docs = all_meta[:, 0].reshape(-1)
    all_places = (all_meta[:, 1] * 256 + all_meta[:, 2]).reshape(-1)
    cos, sin, feats = tables(all_docs, all_places)
    slot = jnp.arange(128) % 64
    query_feats = jnp.where((slot < 3)[None, :] & (docs[:, None] != slot[None, :]), -1e30, 0.0).astype(BF)

    n_down = down_weight.shape[0]
    ring_b = n_down % 16 == 0
    if ring_b:
        wide = core_half(in_weight, core)
        parts_b = [core_half(out_weight, core)] + [wide[:, j : j + 384] for j in range(0, wide.shape[1], 384)]
        piece_b = jnp.concatenate(parts_b + [core_half(down_weight, core)], axis=0)
        piece_b, _ = lax.optimization_barrier((piece_b, pieces[-1]))
        steps_b = list(gather_steps(piece_b, F, C))
    else:
        steps_b = []
    h_all, query, key, value, w_qkv = project(xs, gain_one, own_a, got_a, idx, cos, sin, rows, F)
    pairs = width // 128
    calls = 3
    per = pairs // calls
    ahead = [
        attend(query, key, value, feats, query_feats, steps_b[i + 1][0] if i + 1 < len(steps_b) else query_feats, i * per, per)
        for i in range(calls)
    ]
    mixed_low = jnp.concatenate([a[1] for a in ahead], axis=1)
    if ring_b:
        own_b, got_b = both_cores([p for step in steps_b for p in step], F, C)
        places = [(0, n, 0, 384, 0)]
        places += [(n * (1 + j), n, 1, wide.shape[1], 384 * j) for j in range(wide.shape[1] // 384)]
        places += [(piece_b.shape[0] - n_down, n_down, 2, 384, 0)]
        shapes = [(width, width), (width, in_weight.shape[1]), (n_down * F, width)]
        w_out, w_in, w_down = unpack(own_b, got_b, idx, F, places, shapes)
    else:
        w_out, w_in, w_down = [
            lax.all_gather(w, "fsdp", axis=0, tiled=True) for w in (out_weight, in_weight, down_weight)
        ]

    resid_in = inputs.astype(F32)
    resid = resid_in + nn(mixed_low, w_out)
    normed_two, inv_two = normalize(resid)
    h_two = (normed_two * gain_two).astype(BF)
    ff = w_down.shape[0]
    up_all = nn(h_two, w_in)
    gate, up = up_all[:, :ff], up_all[:, ff:]
    cdf = 0.5 * (1.0 + lax.erf(gate * math.sqrt(0.5)))
    pdf = jnp.exp(-0.5 * gate * gate) * (1.0 / math.sqrt(2.0 * math.pi))
    gelu = gate * cdf
    mid = (gelu * up).astype(BF)
    out = (resid + nn(mid, w_down)).astype(BF).reshape(hidden_in.shape)
    branch = out_cot.reshape(rows, width)
    grad_down = tn(mid, branch)
    grad_mid = nt(branch, w_down)
    grad_u = jnp.concatenate([grad_mid * up * (cdf + gate * pdf), grad_mid * gelu], axis=1).astype(BF)
    grad_in = tn(h_two, grad_u)
    grad_h_two = nt(grad_u, w_in)
    grad_resid = branch.astype(F32) + norm_back(grad_h_two, normed_two, inv_two, gain_two)
    grad_attn = grad_resid.astype(BF)
    grad_out = tn(mixed_low, grad_attn)
    grad_mixed = nt(grad_attn, w_out)

    sum_b = reduce_steps([grad_down, grad_in, grad_out], F, C)
    marks = [next(sum_b) for _ in range(calls)]
    parts = [
        attend_back(
            query, key, value, feats, query_feats, ahead[i][2], ahead[i][3], ahead[i][0], grad_mixed, cos, sin,
            marks[i], i * per, per,
        )
        for i in range(calls)
    ]
    g_down, g_in, g_out = finish(sum_b)
    g_query = jnp.concatenate([p[0] for p in parts], axis=1)
    g_kv = jnp.concatenate([p[1] for p in parts] + [p[2] for p in parts], axis=1)
    h_own = h_all[:rows]
    grad_qkv = jnp.concatenate([tn(h_own, g_query), tn(h_all, g_kv)], axis=1)
    (g_qkv,) = finish(reduce_steps([grad_qkv], F, C))
    grad_h = nt(g_kv, w_qkv[:, width:]).reshape(C, rows, width)
    own_h = nt(g_query, w_qkv[:, :width])
    grad_h_one = reduce_ctx(grad_h, F, C) + own_h
    normed_one, inv_one = normalize(resid_in)
    in_grad = (grad_resid + norm_back(grad_h_one, normed_one, inv_one, gain_one)).reshape(hidden_in.shape)
    g_gain_one = jnp.sum(g_qkv * qkv_weight.astype(F32), axis=1) / norm1_gain.astype(F32)
    g_gain_two = jnp.sum(g_in * in_weight.astype(F32), axis=1) / norm2_gain.astype(F32)
    return (out, in_grad, g_gain_one, g_qkv, g_out, g_gain_two, g_in, g_down)


def solution(mesh):
    F, C = mesh.shape["fsdp"], mesh.shape["ctx"]
    tokens = P("fsdp", "ctx", None)
    ids = P("fsdp", "ctx")
    vec = P("fsdp")
    mat = P("fsdp", None)
    return jax.shard_map(
        functools.partial(body, F, C),
        mesh=mesh,
        in_specs=(tokens, ids, ids, vec, mat, mat, vec, mat, mat, tokens),
        out_specs=(tokens, tokens, vec, mat, mat, vec, mat, mat),
        check_vma=False,
    )
```

```python
import functools
import math

import jax
import jax.numpy as jnp
from jax import lax
from jax.experimental import pallas as pl
from jax.experimental.pallas import tpu as pltpu
from jax.sharding import PartitionSpec as P

HEAD_DIM = 64
rope_base = 160000.0
norm_eps = 1e-05
BF = jnp.bfloat16
F32 = jnp.float32
AXES = ("fsdp", "ctx")
EXP_SCALE = HEAD_DIM ** (-0.5) * math.log2(math.e)
MIB = 2**20


def nt(a, b):
    return lax.dot_general(a, b, (((1,), (1,)), ((), ())), preferred_element_type=F32)


def nn(a, b):
    return lax.dot_general(a, b, (((1,), (0,)), ((), ())), preferred_element_type=F32)


def tn(a, b):
    return lax.dot_general(a, b, (((0,), (0,)), ((), ())), preferred_element_type=F32)


def lanes(shape):
    return lax.broadcasted_iota(jnp.int32, shape, 1)


def split3(v):
    hi = v.astype(BF).astype(F32)
    rest = v - hi
    mid = rest.astype(BF).astype(F32)
    low = (rest - mid).astype(BF).astype(F32)
    return hi, mid, low


def swap_halves(u, lane):
    width = u.shape[1]
    return jnp.where((lane % 64) < 32, pltpu.roll(u, width - 32, 1), pltpu.roll(u, 32, 1))


def permute(x, fn, F, C):
    return lax.ppermute(x, AXES, [(i, fn(i)) for i in range(F * C)])


def after(x, *others):
    return lax.optimization_barrier((x,) + others)[0]


def beside(x, hold):
    return x if hold is None else after(x, *(hold if isinstance(hold, tuple) else (hold,)))


def flip_ctx(x, bit, F, C):
    return permute(x, lambda i: (i // C) * C + ((i % C) ^ bit), F, C)


def flip_fsdp(x, F, C):
    return permute(x, lambda i: (((i // C) ^ 1) * C) + i % C, F, C)


def ring(x, F, C):
    return permute(x, lambda i: (i + 2 * C) % (F * C), F, C)


def ctx_bits(C):
    bits = []
    b = C // 2
    while b:
        bits.append(b)
        b //= 2
    return bits


def gather_ctx(x, F, C):
    have = x[None]
    bits = ctx_bits(C)
    for b in bits[:-1]:
        have = jnp.concatenate([have, flip_ctx(have, b, F, C)], axis=0)
    return have, flip_ctx(have, bits[-1], F, C)


def reduce_ctx(parts, bits, F, C):
    for b in reversed(bits):
        half = parts.shape[0] // 2
        got = flip_ctx(parts[half:].astype(BF), b, F, C)
        parts = parts[:half] + got.astype(F32)
    return parts[0]


def reduce_steps(give, keep, spots, shapes, F, C):
    core = lax.axis_index("ctx") % 2
    me = lax.axis_index("fsdp")
    Z = F // 2
    z, xx = me // 2, me % 2
    hold = yield give
    got = beside(flip_ctx(give, 1, F, C), hold)
    ring_order = [lax.rem(z - 1 - s + Z, Z) * 2 for s in range(Z)]
    order = [d + side for d in ring_order for side in (xx, 1 - xx)]
    acc = add_sorted(keep, got, order)
    hold = yield acc[1]
    total = None
    for s in range(Z):
        give = acc[2 * s + 1]
        got = beside(flip_fsdp(give if s == 0 else after(give, send), F, C), hold)
        mine = acc[2 * s].astype(F32) + got.astype(F32)
        total = mine if total is None else mine + arrived.astype(F32)
        if s < Z - 1:
            send = total.astype(BF)
            hold = yield send
            arrived = ring(send, F, C)
    for b in ctx_bits(C)[:-1]:
        send = total.astype(BF)
        hold = yield send
        total = total + beside(flip_ctx(send, b, F, C), hold).astype(F32)
    send = total.astype(BF)
    hold = yield send
    other = beside(flip_ctx(send, 1, F, C), hold)
    yield spread(total, other, core, spots, shapes)


def finish(steps, hold=None):
    last = next(steps) if hold is None else steps.send(hold)
    for last in steps:
        pass
    return last


def place_pieces(idx_ref, chunks, outs, places, sems, F):
    made = []
    at = 0
    for own_ref, got_ref, count in chunks:
        piece = own_ref.shape[0] // count
        for j in range(count):
            for side, src in ((0, own_ref), (1, got_ref)):
                for row, n, o, half, col, wide in places:
                    r = pl.multiple_of(idx_ref[at + j] * n, n)
                    c = pl.multiple_of(idx_ref[F + side] * half + col, 128)
                    made.append(
                        pltpu.make_async_copy(
                            src.at[pl.ds(j * piece + row, n), :],
                            outs[o].at[pl.ds(r, n), pl.ds(c, wide)],
                            sems.at[len(made)],
                        )
                    )
        at += count
    return made


def unpack_kernel(idx_ref, a_ref, b_ref, c_ref, d_ref, *refs, F, places, counts):
    chunks = [(a_ref, b_ref, counts[0]), (c_ref, d_ref, counts[1])]
    made = place_pieces(idx_ref, chunks, refs[:-1], places, refs[-1], F)
    for c in made:
        c.start()
    for c in made:
        c.wait()


def unpack(chunks, idx, F, places, shapes):
    anywhere = pl.BlockSpec(memory_space=pl.ANY)
    return pl.pallas_call(
        functools.partial(unpack_kernel, F=F, places=places, counts=[c[2] for c in chunks]),
        in_specs=[pl.BlockSpec(memory_space=pltpu.SMEM)] + [anywhere] * 4,
        out_specs=[pl.BlockSpec(memory_space=pltpu.VMEM)] * len(shapes),
        out_shape=[jax.ShapeDtypeStruct(s, BF) for s in shapes],
        scratch_shapes=[pltpu.SemaphoreType.DMA((2 * F * len(places),))],
        compiler_params=pltpu.CompilerParams(vmem_limit_bytes=32 * MIB),
        name="unpack",
    )(idx, chunks[0][0], chunks[0][1], chunks[1][0], chunks[1][1])


def pieces_of(grads, F):
    spots = []
    row = 0
    for g, (rows, cols) in enumerate(grads):
        n = rows // F
        for j in range(0, cols // 2, 384):
            spots.append((g, n, row, 0, 384, j, cols // 2 + j))
            row += n
    return spots, row


def add_sorted_kernel(idx_ref, keep_ref, got_ref, *outs):
    for j, out in enumerate(outs):
        i = idx_ref[j]
        out[...] = (keep_ref[i].astype(F32) + got_ref[i].astype(F32)).astype(BF)


def add_sorted(keep, got, order):
    vmem = pl.BlockSpec(memory_space=pltpu.VMEM)
    return pl.pallas_call(
        add_sorted_kernel,
        in_specs=[pl.BlockSpec(memory_space=pltpu.SMEM), vmem, vmem],
        out_specs=[vmem] * len(order),
        out_shape=[jax.ShapeDtypeStruct(keep.shape[1:], BF)] * len(order),
        compiler_params=pltpu.CompilerParams(vmem_limit_bytes=32 * MIB),
        name="add_sorted",
    )(jnp.stack(order).astype(jnp.int32), keep, got)


def spread_kernel(core_ref, own_ref, other_ref, *outs, spots):
    def write(side):
        for g, n, row, at, wide, *cols in spots:
            c, d = cols[side], cols[1 - side]
            outs[g][:, c : c + wide] = own_ref[row : row + n, at : at + wide]
            outs[g][:, d : d + wide] = other_ref[row : row + n, at : at + wide].astype(F32)

    pl.when(core_ref[0] == 0)(lambda: write(0))
    pl.when(core_ref[0] == 1)(lambda: write(1))


def spread(own, other, core, spots, shapes):
    vmem = pl.BlockSpec(memory_space=pltpu.VMEM)
    return pl.pallas_call(
        functools.partial(spread_kernel, spots=spots),
        in_specs=[pl.BlockSpec(memory_space=pltpu.SMEM), vmem, vmem],
        out_specs=[vmem] * len(shapes),
        out_shape=[jax.ShapeDtypeStruct(s, F32) for s in shapes],
        name="spread",
    )(core.reshape(1), own, other)


def project_kernel(idx_ref, x_ref, y_ref, a_ref, b_ref, c_ref, d_ref, cos_ref, sin_ref, h_ref, q_ref, k_ref, v_ref, w_ref, sems, *, F, n, counts):
    width, rows = h_ref.shape
    half = w_ref.shape[1] // 2
    chunks = [(a_ref, b_ref, counts[0]), (c_ref, d_ref, counts[1])]
    made = place_pieces(idx_ref, chunks, [w_ref], [(0, n, 0, half, 0, half)], sems, F)

    @pl.when(pl.program_id(0) == 0)
    def _():
        for c in made:
            c.start()

    x = jnp.where(pl.program_id(0) < pl.num_programs(0) // 2, x_ref[0, :rows, :], y_ref[0, :rows, :]).astype(F32)
    centred = x - jnp.mean(x, axis=1, keepdims=True)
    var = jnp.mean(centred * centred, axis=1, keepdims=True)
    h = (centred * lax.rsqrt(var + norm_eps)).astype(BF)
    h_ref[...] = h.T

    @pl.when(pl.program_id(0) == 0)
    def _():
        for c in made:
            c.wait()

    cos, sin = cos_ref[...], sin_ref[...]
    lane = lanes((rows, 128))

    def rope_into(ref, offset):
        for j in range(0, width, 256):
            u = nn(h, w_ref[:, offset + j : offset + j + 256])
            for i in (0, 128):
                t = u[:, i : i + 128]
                ref[:, j + i : j + i + 128] = (t * cos + swap_halves(t, lane) * sin).astype(BF)

    rope_into(k_ref, width)
    for j in range(0, width, 256):
        v_ref[:, j : j + 256] = nn(h, w_ref[:, 2 * width + j : 2 * width + j + 256]).astype(BF)

    @pl.when(pl.program_id(0) == 0)
    def _():
        rope_into(q_ref, 0)


def project(xs, chunks, idx, cos, sin, rows, F):
    near, far = xs
    C, width = 2 * near.shape[0], near.shape[2]
    blk = pl.BlockSpec((rows, width), lambda i: (i, 0))
    tab = pl.BlockSpec((rows, 128), lambda i: (i, 0))
    whole = lambda i: (0, 0)
    out = jax.ShapeDtypeStruct((C * rows, width), BF)
    return pl.pallas_call(
        functools.partial(project_kernel, F=F, n=width // F, counts=[c[2] for c in chunks]),
        grid=(C,),
        in_specs=[
            pl.BlockSpec(memory_space=pltpu.SMEM),
            pl.BlockSpec((1,) + near.shape[1:], lambda i: (jnp.minimum(i, C // 2 - 1), 0, 0)),
            pl.BlockSpec((1,) + near.shape[1:], lambda i: (jnp.maximum(i - C // 2, 0), 0, 0)),
        ]
        + [pl.BlockSpec(memory_space=pl.ANY)] * 4
        + [tab, tab],
        out_specs=[
            pl.BlockSpec((width, rows), lambda i: (0, i)),
            pl.BlockSpec((rows, width), whole),
            blk,
            blk,
            pl.BlockSpec((width, 3 * width), whole),
        ],
        out_shape=[jax.ShapeDtypeStruct((width, C * rows), BF), jax.ShapeDtypeStruct((rows, width), BF), out, out, jax.ShapeDtypeStruct((width, 3 * width), BF)],
        scratch_shapes=[pltpu.SemaphoreType.DMA((2 * F,))],
        compiler_params=pltpu.CompilerParams(vmem_limit_bytes=40 * MIB),
        name="project",
    )(idx, near, far, chunks[0][0], chunks[0][1], chunks[1][0], chunks[1][1], cos, sin)


def forward_kernel(q_ref, k_ref, v_ref, f_ref, fq_ref, *refs, rows, blocks):
    low_ref, stat_ref = refs[-2:]
    lane = lanes((rows, 128))
    low = lane < 64
    q, fq = q_ref[...], fq_ref[...]
    outs = []
    for x in range(2):
        pick = low if x == 0 else ~low
        qx = jnp.where(pick, q, fq)
        acc = None
        for j in range(blocks):
            sl = pl.ds(j * rows, rows)
            f = f_ref[sl, :]
            kx = jnp.where(pick, k_ref[sl, :], f)
            vx = jnp.where(pick, v_ref[sl, :], f)
            s = nt(qx, kx)
            if j == 0:
                top = jnp.max(s, axis=1, keepdims=True)
            p = jnp.exp2((s - top) * EXP_SCALE).astype(BF)
            a = nn(p, vx)
            acc = a if acc is None else acc + a
        at = 70 if x == 0 else 6
        tot = acc[:, at : at + 1]
        outs.append((acc / tot, jnp.where(lane % 64 == 0, top, tot)))
    (a0, s0), (a1, s1) = outs
    low_ref[...] = jnp.where(low, a0, a1).astype(BF)
    stat_ref[...] = jnp.where(low, s0, s1)


def attend(q, k, v, f, fq, after_this, first, n, into):
    rows, T = q.shape[0], k.shape[0]
    qs = pl.BlockSpec((rows, 128), lambda i: (0, i + first))
    ks = pl.BlockSpec((T, 128), lambda i: (0, i + first))
    cf = pl.BlockSpec((T, 128), lambda i: (0, 0))
    cq = pl.BlockSpec((rows, 128), lambda i: (0, 0))
    anywhere = pl.BlockSpec(memory_space=pl.ANY)
    into = [] if into is None else list(into)
    return pl.pallas_call(
        functools.partial(forward_kernel, rows=rows, blocks=T // rows),
        grid=(n,),
        in_specs=[qs, ks, ks, cf, cq, anywhere] + [anywhere] * len(into),
        out_specs=[qs, qs],
        out_shape=[jax.ShapeDtypeStruct(q.shape, BF), jax.ShapeDtypeStruct(q.shape, F32)],
        input_output_aliases={6 + i: i for i in range(len(into))},
        compiler_params=pltpu.CompilerParams(vmem_limit_bytes=40 * MIB),
        name="attend",
    )(q, k, v, f, fq, after_this, *into)


def backward_kernel(q_ref, k_ref, v_ref, f_ref, fq_ref, stat_ref, mix_ref, gm_ref, cos_ref, sin_ref, *refs, rows, blocks):
    dq_ref, dk_ref, dv_ref, sk_ref, sv_ref = refs[-5:]
    lane = lanes((rows, 128))
    low = lane < 64
    slot = lane % 64
    q = q_ref[...]
    stat = stat_ref[...]
    tot = jnp.where(low, stat[:, 1:2], stat[:, 65:66])
    ga = gm_ref[...] / tot
    prod = ga * mix_ref[...].astype(F32)
    hi, mid, lo = split3(jnp.where(low, stat[:, 64:65], stat[:, 0:1]))
    fq = jnp.where(slot == 3, -hi, jnp.where(slot == 4, -mid, jnp.where(slot == 5, -lo, fq_ref[...].astype(F32)))).astype(BF)
    gab = ga.astype(BF)
    dqs = []
    for x in range(2):
        pick = low if x == 0 else ~low
        qx = jnp.where(pick, q, fq)
        delta = jnp.sum(jnp.where(pick, prod, 0.0), axis=1, keepdims=True)
        h3, m3, l3 = split3(jnp.broadcast_to(delta, (rows, 128)))
        gf = jnp.where(slot == 6, -h3, jnp.where(slot == 7, -m3, jnp.where(slot == 8, -l3, 0.0))).astype(BF)
        gx = jnp.where(pick, gab, gf)
        gxt = gx.T[64 * x : 64 * x + 64]
        qxt = qx.T[64 * x : 64 * x + 64]
        dq = None
        for j in range(blocks):
            sl = pl.ds(j * rows, rows)
            f = f_ref[sl, :]
            kx = jnp.where(pick, k_ref[sl, :], f)
            vx = jnp.where(pick, v_ref[sl, :], f)
            p = jnp.exp2(nt(qx, kx) * EXP_SCALE)
            ds = (p * nt(gx, vx)).astype(BF)
            d = nn(ds, kx)
            dq = d if dq is None else dq + d
            sv_ref[64 * x : 64 * x + 64, sl] = nn(gxt, p.astype(BF))
            sk_ref[64 * x : 64 * x + 64, sl] = nn(qxt, ds)
        dqs.append(dq)
    scale = HEAD_DIM ** (-0.5)

    def unrope(u, sl):
        return (u * cos_ref[sl, :] - swap_halves(u, lane) * sin_ref[sl, :]).astype(BF)

    dq_ref[...] = unrope(jnp.where(low, dqs[0], dqs[1]) * scale, pl.ds(0, rows))
    for j in range(blocks):
        sl = pl.ds(j * rows, rows)
        dv_ref[sl, :] = sv_ref[:, sl].T.astype(BF)
        dk_ref[sl, :] = unrope(sk_ref[:, sl].T * scale, sl)


def attend_back(q, k, v, f, fq, stat, mix, gm, cos, sin, after_this, first, n):
    rows, T = q.shape[0], k.shape[0]
    qs = pl.BlockSpec((rows, 128), lambda i: (0, i + first))
    ks = pl.BlockSpec((T, 128), lambda i: (0, i + first))
    cf = pl.BlockSpec((T, 128), lambda i: (0, 0))
    cq = pl.BlockSpec((rows, 128), lambda i: (0, 0))
    oq = pl.BlockSpec((rows, 128), lambda i: (0, i))
    ok = pl.BlockSpec((T, 128), lambda i: (0, i))
    return pl.pallas_call(
        functools.partial(backward_kernel, rows=rows, blocks=T // rows),
        grid=(n,),
        in_specs=[qs, ks, ks, cf, cq, qs, qs, qs, cf, cf, pl.BlockSpec(memory_space=pl.ANY)],
        out_specs=[oq, ok, ok],
        out_shape=[jax.ShapeDtypeStruct((rows, 128 * n), BF)] + [jax.ShapeDtypeStruct((T, 128 * n), BF)] * 2,
        scratch_shapes=[pltpu.VMEM((128, T), F32), pltpu.VMEM((128, T), F32)],
        compiler_params=pltpu.CompilerParams(vmem_limit_bytes=48 * MIB),
        name="attend_back",
    )(q, k, v, f, fq, stat, mix, gm, cos, sin, after_this)


def mlp_grads_kernel(core_ref, mid_ref, h_ref, mix_ref, branch_ref, gu_ref, ga_ref, give_ref, keep_ref, mid_t, h_t, mix_t, *, F, spots):
    step = pl.program_id(0)

    @pl.when(step == 0)
    def _():
        mid_t[...] = mid_ref[...].T
        h_t[...] = h_ref[...].T
        mix_t[...] = mix_ref[...].T

    def run(out_ref):
        for left, right, mine in ((mid_t, branch_ref, 0), (h_t, gu_ref, 1), (mix_t, ga_ref, 2)):
            for g, n, row, _, wide, col, _ in spots:
                if g == mine:
                    r = nn(left[...], right[:, col : col + wide]).astype(BF)
                    for p in range(F):
                        out_ref[p, row : row + n, :] = r[p * n : (p + 1) * n]

    pl.when(step == 0)(lambda: run(give_ref))
    pl.when(step == 1)(lambda: run(keep_ref))


def mlp_grads(mid, h, mix, branch, gu, ga, core, F, spots, R):
    rows = mid.shape[0]
    half = lambda i, c: (0, 1 - c[0] + i * (2 * c[0] - 1))
    whole = lambda i, c: (0, 0)
    piece = pl.BlockSpec((F, R, 384), lambda i, c: (0, 0, 0))
    out = jax.ShapeDtypeStruct((F, R, 384), BF)
    return pl.pallas_call(
        functools.partial(mlp_grads_kernel, F=F, spots=spots),
        grid_spec=pltpu.PrefetchScalarGridSpec(
            num_scalar_prefetch=1,
            grid=(2,),
            in_specs=[pl.BlockSpec(a.shape, whole) for a in (mid, h, mix)]
            + [pl.BlockSpec((rows, a.shape[1] // 2), half) for a in (branch, gu, ga)],
            out_specs=[piece, piece],
            scratch_shapes=[pltpu.VMEM(a.shape[::-1], BF) for a in (mid, h, mix)],
        ),
        out_shape=[out, out],
        compiler_params=pltpu.CompilerParams(vmem_limit_bytes=40 * MIB),
        name="mlp_grads",
    )(core.reshape(1), mid, h, mix, branch, gu, ga)


def qkv_grads_kernel(core_ref, ht_ref, *refs, F):
    give_ref, keep_ref = refs[-2:]
    parts = refs[:-2]
    count = len(parts) // 3
    width = ht_ref.shape[0]
    n = width // F

    def run(out_ref):
        for g in range(3):
            right = jnp.concatenate([parts[g * count + i][...] for i in range(count)], axis=1)
            r = nn(ht_ref[:, : right.shape[0]], right).astype(BF)
            for p in range(F):
                out_ref[p, g * n : (g + 1) * n, :] = r[p * n : (p + 1) * n]

    step = pl.program_id(0)
    pl.when(step == 0)(lambda: run(give_ref))
    pl.when(step == 1)(lambda: run(keep_ref))


def qkv_grads(ht, parts, core, F):
    width, T = ht.shape
    half = lambda i, c: (0, 1 - c[0] + i * (2 * c[0] - 1))
    piece = pl.BlockSpec((F, 3 * width // F, width // 2), lambda i, c: (0, 0, 0))
    out = jax.ShapeDtypeStruct((F, 3 * width // F, width // 2), BF)
    return pl.pallas_call(
        functools.partial(qkv_grads_kernel, F=F),
        grid_spec=pltpu.PrefetchScalarGridSpec(
            num_scalar_prefetch=1,
            grid=(2,),
            in_specs=[pl.BlockSpec((width, T), lambda i, c: (0, 0))] + [pl.BlockSpec((a.shape[0], 128), half) for a in parts],
            out_specs=[piece, piece],
        ),
        out_shape=[out, out],
        compiler_params=pltpu.CompilerParams(vmem_limit_bytes=52 * MIB),
        name="qkv_grads",
    )(core.reshape(1), ht, *parts)


def grad_h_kernel(after_ref, w_ref, *refs, count, own):
    out_ref = refs[-1]
    width = out_ref.shape[1]
    wide = width // count

    def product(which, offset):
        total = None
        for i in range(count):
            c = offset + i * wide
            r = nt(refs[which * count + i][...], w_ref[:, c : c + wide])
            total = r if total is None else total + r
        return total

    out_ref[...] = (product(1, width) + product(2, 2 * width)).astype(out_ref.dtype)
    if own:

        @pl.when(pl.program_id(0) == 0)
        def _():
            out_ref[...] += product(0, 0)


def grad_h(parts, w, first, blocks, dtype, own, after_this):
    count = len(parts) // 3
    rows, width = parts[0].shape[0], w.shape[0]
    return pl.pallas_call(
        functools.partial(grad_h_kernel, count=count, own=own),
        grid=(blocks,),
        in_specs=[pl.BlockSpec(memory_space=pl.ANY), pl.BlockSpec(w.shape, lambda i: (0, 0))]
        + [pl.BlockSpec(a.shape, lambda i: (0, 0)) for a in parts[:count]]
        + [pl.BlockSpec((rows, a.shape[1]), lambda i: (i + first, 0)) for a in parts[count:]],
        out_specs=pl.BlockSpec((rows, width), lambda i: (i, 0)),
        out_shape=jax.ShapeDtypeStruct((blocks * rows, width), dtype),
        compiler_params=pltpu.CompilerParams(vmem_limit_bytes=40 * MIB),
        name="grad_h",
    )(after_this, w, *parts)


def normalize(fields):
    centred = fields - jnp.mean(fields, axis=-1, keepdims=True)
    variance = jnp.mean(centred * centred, axis=-1, keepdims=True)
    inv_root = lax.rsqrt(variance + norm_eps)
    return centred * inv_root, inv_root


def norm_back(scaled, normed, inv_root):
    return inv_root * (
        scaled
        - jnp.mean(scaled, axis=-1, keepdims=True)
        - normed * jnp.mean(scaled * normed, axis=-1, keepdims=True)
    )


def tables(docs, places):
    lane = jnp.arange(128)
    frequency = rope_base ** (-2.0 * (lane % 32).astype(F32) / HEAD_DIM)
    angles = places.astype(F32)[:, None] * frequency[None, :]
    sign = jnp.where(lane % 64 < 32, -1.0, 1.0)
    slot = lane % 64
    same = (docs[:, None] == slot[None, :]) & (slot < 3)[None, :]
    ones = ((slot >= 3) & (slot < 9))[None, :]
    feats = jnp.where(same | ones, 1.0, 0.0).astype(BF)
    return jnp.cos(angles), jnp.sin(angles) * sign, feats


def core_half(shard, core):
    half = shard.shape[1] // 2
    return lax.dynamic_slice_in_dim(shard, core * half, half, 1)


def gather_steps(piece, pieces, F, C):
    Z = F // 2
    same = piece
    for k in range(Z):
        other = flip_fsdp(same, F, C)
        nxt = ring(same, F, C) if k < Z - 1 else None
        hold = yield same
        if hold is not None:
            other = after(other, hold)
        pieces += [same, other]
        if nxt is not None:
            same = after(nxt, other)


def run_out(steps, hold):
    try:
        steps.send(hold)
        while True:
            next(steps)
    except StopIteration:
        pass


def owners_of(F):
    Z = F // 2
    me = lax.axis_index("fsdp")
    z, xx = me // 2, me % 2
    owners = []
    for k in range(Z):
        base = lax.rem(z - k + Z, Z) * 2
        owners += [base + xx, base + 1 - xx]
    return owners


def both_cores(pieces, F, C):
    chunks = []
    for part in (pieces[:-2], pieces[-2:]):
        own = jnp.concatenate(part[:-1] + [after(part[-1], pieces[-2])], axis=0)
        chunks.append((own, flip_ctx(own, 1, F, C), len(part)))
    return chunks


def body(
    F, C, hidden_in, segment_ids, positions, norm1_gain, qkv_weight, out_weight, norm2_gain, in_weight, down_weight, out_cot
):
    width = hidden_in.shape[-1]
    rows = hidden_in.shape[1]
    inputs = hidden_in.reshape(rows, width)
    docs = segment_ids.reshape(-1)
    places = positions.reshape(-1)
    extra = jnp.zeros((16, width), BF)
    meta = jnp.stack([docs, places // 256, places % 256]).astype(BF)
    extra = lax.dynamic_update_slice(extra, meta, (0, 0))
    xs = gather_ctx(jnp.concatenate([inputs, extra], axis=0), F, C)
    core = lax.axis_index("ctx") % 2
    owners = owners_of(F)
    idx = jnp.stack([jnp.asarray(o, jnp.int32) for o in owners] + [core, 1 - core]).astype(jnp.int32)
    n = width // F
    own_gain_one = norm1_gain.astype(F32)[:, None]
    own_gain_two = norm2_gain.astype(F32)[:, None]
    half = (core_half(qkv_weight, core).astype(F32) * own_gain_one).astype(BF)
    scaled_in = (in_weight.astype(F32) * own_gain_two).astype(BF)
    all_meta = jnp.concatenate([x[:, rows : rows + 3, :rows] for x in xs]).astype(jnp.int32)
    all_docs = all_meta[:, 0].reshape(-1)
    all_places = (all_meta[:, 1] * 256 + all_meta[:, 2]).reshape(-1)
    cos, sin, feats = tables(all_docs, all_places)
    pieces = []
    ring_a = gather_steps(half, pieces, F, C)
    for _ in range(F // 2):
        next(ring_a)
    run_out(ring_a, cos)
    chunks_a = both_cores(pieces, F, C)
    slot = jnp.arange(128) % 64
    query_feats = jnp.where((slot < 3)[None, :] & (docs[:, None] != slot[None, :]), -1e30, 0.0).astype(BF)

    n_down = down_weight.shape[0]
    ring_b = n_down % 16 == 0
    if ring_b:
        wide = core_half(scaled_in, core)
        parts_b = [core_half(out_weight, core)] + [wide[:, j : j + 384] for j in range(0, wide.shape[1], 384)]
        piece_b = jnp.concatenate(parts_b + [core_half(down_weight, core)], axis=0)
        pieces_b = []
        steps_b = gather_steps(after(piece_b, pieces[-1], xs[1]), pieces_b, F, C)
        next(steps_b)
    h_t, query, key, value, w_qkv = project(xs, chunks_a, idx, cos, sin, rows, F)
    pairs = width // 128
    calls = 3
    per = pairs // calls
    mixed = None
    done = query
    for i in range(calls):
        mark = query_feats
        if ring_b:
            mark = steps_b.send(done)
        mixed = attend(query, key, value, feats, query_feats, mark, i * per, per, mixed)
        done = mixed[0]
    mixed_low, stat = mixed
    if ring_b:
        run_out(steps_b, done)
        places = [(0, n, 0, 384, 0, 384)]
        places += [(n * (1 + j), n, 1, wide.shape[1], 384 * j, 384) for j in range(wide.shape[1] // 384)]
        places += [(piece_b.shape[0] - n_down, n_down, 2, 384, 0, 384)]
        shapes = [(width, width), (width, in_weight.shape[1]), (n_down * F, width)]
        w_out, w_in, w_down = unpack(both_cores(pieces_b, F, C), idx, F, places, shapes)
    else:
        w_out, w_in, w_down = [
            lax.all_gather(w, "fsdp", axis=0, tiled=True) for w in (out_weight, scaled_in, down_weight)
        ]

    resid_in = inputs.astype(F32)
    resid = resid_in + nn(mixed_low, w_out)
    normed_two, inv_two = normalize(resid)
    h_two = normed_two.astype(BF)
    ff = w_down.shape[0]
    up_all = nn(h_two, w_in)
    gate, up = up_all[:, :ff], up_all[:, ff:]
    cdf = 0.5 * (1.0 + lax.erf(gate * math.sqrt(0.5)))
    pdf = jnp.exp(-0.5 * gate * gate) * (1.0 / math.sqrt(2.0 * math.pi))
    gelu = gate * cdf
    mid = (gelu * up).astype(BF)
    branch = out_cot.reshape(rows, width)
    grad_mid = nt(branch, w_down)
    grad_u = jnp.concatenate([grad_mid * up * (cdf + gate * pdf), grad_mid * gelu], axis=1).astype(BF)
    grad_h_two = nt(grad_u, w_in)
    grad_resid = branch.astype(F32) + norm_back(grad_h_two, normed_two, inv_two)
    grad_attn = grad_resid.astype(BF)
    grad_mixed = nt(grad_attn, w_out)

    shapes_b = [(ff, width), (width, 2 * ff), (width, width)]
    spots_b, rows_b = pieces_of(shapes_b, F)
    give_b, keep_b = mlp_grads(mid, h_two, mixed_low, branch, grad_u, grad_attn, core, F, spots_b, rows_b)
    sum_b = reduce_steps(give_b, keep_b, spots_b, [(r // F, c) for r, c in shapes_b], F, C)
    back = []
    mark = next(sum_b)
    for i in range(calls):
        back.append(
            attend_back(query, key, value, feats, query_feats, stat, mixed_low, grad_mixed, cos, sin, mark, i * per, per)
        )
        mark = sum_b.send(back[-1][0])
    parts = [b[g] for g in range(3) for b in back]
    give_a, keep_a = qkv_grads(h_t, [after(parts[0], mark)] + parts[1:], core, F)
    sent_b = sum_b.send(give_a)
    spots_a = [
        (0, n, g * n, 128 * i, 128, g * width + 256 * i, g * width + 256 * i + 128) for g in range(3) for i in range(calls)
    ]
    sum_a = reduce_steps(after(give_a, sent_b), keep_a, spots_a, [(n, 3 * width)], F, C)
    next(sum_a)
    far = C // 2
    send_h = grad_h(parts, w_qkv, far, far, BF, False, sent_b)
    acc_a = sum_a.send(send_h)
    near = grad_h(parts, w_qkv, 0, far, F32, True, acc_a)
    stage_b = sum_b.send(near)
    stage_a = sum_a.send(stage_b)
    got_h = after(flip_ctx(send_h, 1, F, C), stage_a).astype(F32)
    near = near + got_h
    out = (resid + nn(after(mid, stage_a), w_down)).astype(BF).reshape(hidden_in.shape)
    stage_a = sum_a.send((out, near))
    stage_b = sum_b.send(stage_a)
    stage_a = sum_a.send(stage_b)
    g_down, g_in, g_out = finish(sum_b, stage_a)
    grad_h_one = after(reduce_ctx(near.reshape(far, rows, width), ctx_bits(C)[:-1], F, C), stage_a)
    normed_one, inv_one = normalize(after(inputs, stage_a).astype(F32))
    in_grad = (grad_resid + norm_back(grad_h_one, normed_one, inv_one)).reshape(hidden_in.shape)
    g_gain_two = jnp.sum(g_in * in_weight.astype(F32), axis=1)
    g_in = g_in * own_gain_two
    (g_qkv,) = finish(sum_a, (in_grad, g_in, g_gain_two))
    g_gain_one = jnp.sum(g_qkv * qkv_weight.astype(F32), axis=1)
    g_qkv = g_qkv * own_gain_one
    return (out, in_grad, g_gain_one, g_qkv, g_out, g_gain_two, g_in, g_down)


def solution(mesh):
    F, C = mesh.shape["fsdp"], mesh.shape["ctx"]
    tokens = P("fsdp", "ctx", None)
    ids = P("fsdp", "ctx")
    vec = P("fsdp")
    mat = P("fsdp", None)
    return jax.shard_map(
        functools.partial(body, F, C),
        mesh=mesh,
        in_specs=(tokens, ids, ids, vec, mat, mat, vec, mat, mat, tokens),
        out_specs=(tokens, tokens, vec, mat, mat, vec, mat, mat),
        check_vma=False,
    )
```

```python
import functools
import math

import jax
import jax.numpy as jnp
from jax import lax
from jax.experimental import pallas as pl
from jax.experimental.pallas import tpu as pltpu
from jax.sharding import PartitionSpec as P

HEAD_DIM = 64
rope_base = 160000.0
norm_eps = 1e-05
BF = jnp.bfloat16
F32 = jnp.float32
AXES = ("fsdp", "ctx")
EXP_SCALE = HEAD_DIM ** (-0.5) * math.log2(math.e)
MIB = 2**20


def nt(a, b):
    return lax.dot_general(a, b, (((1,), (1,)), ((), ())), preferred_element_type=F32)


def nn(a, b):
    return lax.dot_general(a, b, (((1,), (0,)), ((), ())), preferred_element_type=F32)


def tn(a, b):
    return lax.dot_general(a, b, (((0,), (0,)), ((), ())), preferred_element_type=F32)


def lanes(shape):
    return lax.broadcasted_iota(jnp.int32, shape, 1)


def split3(v):
    hi = v.astype(BF).astype(F32)
    rest = v - hi
    mid = rest.astype(BF).astype(F32)
    low = (rest - mid).astype(BF).astype(F32)
    return hi, mid, low


def swap_halves(u, lane):
    width = u.shape[1]
    return jnp.where((lane % 64) < 32, pltpu.roll(u, width - 32, 1), pltpu.roll(u, 32, 1))


def permute(x, fn, F, C):
    return lax.ppermute(x, AXES, [(i, fn(i)) for i in range(F * C)])


def after(x, *others):
    return lax.optimization_barrier((x,) + others)[0]


def beside(x, hold):
    return x if hold is None else after(x, *(hold if isinstance(hold, tuple) else (hold,)))


def flip_ctx(x, bit, F, C):
    return permute(x, lambda i: (i // C) * C + ((i % C) ^ bit), F, C)


def flip_fsdp(x, F, C):
    return permute(x, lambda i: (((i // C) ^ 1) * C) + i % C, F, C)


def ring(x, F, C):
    return permute(x, lambda i: (i + 2 * C) % (F * C), F, C)


def ctx_bits(C):
    bits = []
    b = C // 2
    while b:
        bits.append(b)
        b //= 2
    return bits


def gather_ctx(x, hold, F, C):
    have = x[None]
    bits = ctx_bits(C)
    for b in bits[:-1]:
        have = jnp.concatenate([have, after(flip_ctx(have, b, F, C), hold)], axis=0)
    return have, flip_ctx(have, bits[-1], F, C)


def reduce_ctx(parts, bits, F, C):
    for b in reversed(bits):
        half = parts.shape[0] // 2
        got = flip_ctx(parts[half:].astype(BF), b, F, C)
        parts = parts[:half] + got.astype(F32)
    return parts[0]


def reduce_steps(give, keep, spots, shapes, scaled, F, C):
    core = lax.axis_index("ctx") % 2
    me = lax.axis_index("fsdp")
    Z = F // 2
    z, xx = me // 2, me % 2
    hold = yield give
    got = beside(flip_ctx(give, 1, F, C), hold)
    ring_order = [lax.rem(z - 1 - s + Z, Z) * 2 for s in range(Z)]
    order = [d + side for d in ring_order for side in (xx, 1 - xx)]
    acc = add_sorted(keep, got, order)
    hold = yield acc[1]
    total = None
    for s in range(Z):
        give = acc[2 * s + 1]
        got = beside(flip_fsdp(give if s == 0 else after(give, send), F, C), hold)
        mine = acc[2 * s].astype(F32) + got.astype(F32)
        total = mine if total is None else mine + arrived.astype(F32)
        if s < Z - 1:
            send = total.astype(BF)
            hold = yield send
            arrived = ring(send, F, C)
    for b in ctx_bits(C)[:-1]:
        send = total.astype(BF)
        hold = yield send
        total = total + beside(flip_ctx(send, b, F, C), hold).astype(F32)
    send = total.astype(BF)
    hold = yield send
    other = beside(flip_ctx(send, 1, F, C), hold)
    yield spread(total, other, core, spots, shapes, scaled)


def finish(steps, hold=None):
    last = next(steps) if hold is None else steps.send(hold)
    for last in steps:
        pass
    return last


def place_pieces(idx_ref, chunks, outs, places, sems, F):
    made = []
    at = 0
    for own_ref, got_ref, count in chunks:
        piece = own_ref.shape[0] // count
        for j in range(count):
            for side, src in ((0, own_ref), (1, got_ref)):
                for row, n, o, half, col, wide in places:
                    r = pl.multiple_of(idx_ref[at + j] * n, n)
                    c = pl.multiple_of(idx_ref[F + side] * half + col, 128)
                    made.append(
                        pltpu.make_async_copy(
                            src.at[pl.ds(j * piece + row, n), :],
                            outs[o].at[pl.ds(r, n), pl.ds(c, wide)],
                            sems.at[len(made)],
                        )
                    )
        at += count
    return made


def unpack_kernel(idx_ref, a_ref, b_ref, c_ref, d_ref, *refs, F, places, counts):
    chunks = [(a_ref, b_ref, counts[0]), (c_ref, d_ref, counts[1])]
    made = place_pieces(idx_ref, chunks, refs[:-1], places, refs[-1], F)
    for c in made:
        c.start()
    for c in made:
        c.wait()


def unpack(chunks, idx, F, places, shapes):
    anywhere = pl.BlockSpec(memory_space=pl.ANY)
    return pl.pallas_call(
        functools.partial(unpack_kernel, F=F, places=places, counts=[c[2] for c in chunks]),
        in_specs=[pl.BlockSpec(memory_space=pltpu.SMEM)] + [anywhere] * 4,
        out_specs=[pl.BlockSpec(memory_space=pltpu.VMEM)] * len(shapes),
        out_shape=[jax.ShapeDtypeStruct(s, BF) for s in shapes],
        scratch_shapes=[pltpu.SemaphoreType.DMA((2 * F * len(places),))],
        compiler_params=pltpu.CompilerParams(vmem_limit_bytes=32 * MIB),
        name="unpack",
    )(idx, chunks[0][0], chunks[0][1], chunks[1][0], chunks[1][1])


def pieces_of(grads, F):
    spots = []
    row = 0
    for g, (rows, cols) in enumerate(grads):
        n = rows // F
        for j in range(0, cols // 2, 384):
            spots.append((g, n, row, 0, 384, j, cols // 2 + j))
            row += n
    return spots, row


def add_sorted_kernel(idx_ref, keep_ref, got_ref, *outs):
    for j, out in enumerate(outs):
        i = idx_ref[j]
        out[...] = (keep_ref[i].astype(F32) + got_ref[i].astype(F32)).astype(BF)


def add_sorted(keep, got, order):
    vmem = pl.BlockSpec(memory_space=pltpu.VMEM)
    return pl.pallas_call(
        add_sorted_kernel,
        in_specs=[pl.BlockSpec(memory_space=pltpu.SMEM), vmem, vmem],
        out_specs=[vmem] * len(order),
        out_shape=[jax.ShapeDtypeStruct(keep.shape[1:], BF)] * len(order),
        compiler_params=pltpu.CompilerParams(vmem_limit_bytes=32 * MIB),
        name="add_sorted",
    )(jnp.stack(order).astype(jnp.int32), keep, got)


def spread_kernel(core_ref, own_ref, other_ref, *refs, spots, scaled):
    weights = [(refs[2 * i], refs[2 * i + 1]) for i in range(len(scaled))]
    outs = refs[2 * len(scaled) :]

    def write(side):
        for g, n, row, at, wide, *cols in spots:
            c, d = cols[side], cols[1 - side]
            outs[g][:, c : c + wide] = own_ref[row : row + n, at : at + wide]
            outs[g][:, d : d + wide] = other_ref[row : row + n, at : at + wide].astype(F32)

    pl.when(core_ref[0] == 0)(lambda: write(0))
    pl.when(core_ref[0] == 1)(lambda: write(1))
    for (w_ref, gain_ref), g, sum_ref in zip(weights, scaled, outs[len(outs) - len(scaled) :]):
        v = outs[g][...]
        sums = jnp.sum(v * w_ref[...].astype(F32), axis=1, keepdims=True)
        sum_ref[...] = jnp.broadcast_to(sums, (v.shape[0], 128)).T[:1]
        outs[g][...] = v * gain_ref[...]


def spread(own, other, core, spots, shapes, scaled):
    vmem = pl.BlockSpec(memory_space=pltpu.VMEM)
    more = [a for pair in scaled.values() for a in pair]
    outs = [jax.ShapeDtypeStruct(s, F32) for s in shapes]
    outs += [jax.ShapeDtypeStruct((1, shapes[g][0]), F32) for g in scaled]
    return pl.pallas_call(
        functools.partial(spread_kernel, spots=spots, scaled=list(scaled)),
        in_specs=[pl.BlockSpec(memory_space=pltpu.SMEM), vmem, vmem] + [vmem] * len(more),
        out_specs=[vmem] * len(outs),
        out_shape=outs,
        name="spread",
    )(core.reshape(1), own, other, *more)


def project_kernel(idx_ref, x_ref, y_ref, a_ref, b_ref, c_ref, d_ref, cos_ref, sin_ref, h_ref, q_ref, k_ref, v_ref, w_ref, sems, *, F, n, counts):
    width, rows = h_ref.shape
    half = w_ref.shape[1] // 2
    chunks = [(a_ref, b_ref, counts[0]), (c_ref, d_ref, counts[1])]
    made = place_pieces(idx_ref, chunks, [w_ref], [(0, n, 0, half, 0, half)], sems, F)

    @pl.when(pl.program_id(0) == 0)
    def _():
        for c in made:
            c.start()

    x = jnp.where(pl.program_id(0) < pl.num_programs(0) // 2, x_ref[0, :rows, :], y_ref[0, :rows, :]).astype(F32)
    centred = x - jnp.mean(x, axis=1, keepdims=True)
    var = jnp.mean(centred * centred, axis=1, keepdims=True)
    h = (centred * lax.rsqrt(var + norm_eps)).astype(BF)
    h_ref[...] = h.T

    @pl.when(pl.program_id(0) == 0)
    def _():
        for c in made:
            c.wait()

    cos, sin = cos_ref[...], sin_ref[...]
    lane = lanes((rows, 128))

    def rope_into(ref, offset):
        for j in range(0, width, 256):
            u = nn(h, w_ref[:, offset + j : offset + j + 256])
            for i in (0, 128):
                t = u[:, i : i + 128]
                ref[:, j + i : j + i + 128] = (t * cos + swap_halves(t, lane) * sin).astype(BF)

    rope_into(k_ref, width)
    for j in range(0, width, 256):
        v_ref[:, j : j + 256] = nn(h, w_ref[:, 2 * width + j : 2 * width + j + 256]).astype(BF)

    @pl.when(pl.program_id(0) == 0)
    def _():
        rope_into(q_ref, 0)


def project(xs, chunks, idx, cos, sin, rows, F):
    near, far = xs
    C, width = 2 * near.shape[0], near.shape[2]
    blk = pl.BlockSpec((rows, width), lambda i: (i, 0))
    tab = pl.BlockSpec((rows, 128), lambda i: (i, 0))
    whole = lambda i: (0, 0)
    out = jax.ShapeDtypeStruct((C * rows, width), BF)
    return pl.pallas_call(
        functools.partial(project_kernel, F=F, n=width // F, counts=[c[2] for c in chunks]),
        grid=(C,),
        in_specs=[
            pl.BlockSpec(memory_space=pltpu.SMEM),
            pl.BlockSpec((1,) + near.shape[1:], lambda i: (jnp.minimum(i, C // 2 - 1), 0, 0)),
            pl.BlockSpec((1,) + near.shape[1:], lambda i: (jnp.maximum(i - C // 2, 0), 0, 0)),
        ]
        + [pl.BlockSpec(memory_space=pl.ANY)] * 4
        + [tab, tab],
        out_specs=[
            pl.BlockSpec((width, rows), lambda i: (0, i)),
            pl.BlockSpec((rows, width), whole),
            blk,
            blk,
            pl.BlockSpec((width, 3 * width), whole),
        ],
        out_shape=[jax.ShapeDtypeStruct((width, C * rows), BF), jax.ShapeDtypeStruct((rows, width), BF), out, out, jax.ShapeDtypeStruct((width, 3 * width), BF)],
        scratch_shapes=[pltpu.SemaphoreType.DMA((2 * F,))],
        compiler_params=pltpu.CompilerParams(vmem_limit_bytes=60 * MIB),
        name="project",
    )(idx, near, far, chunks[0][0], chunks[0][1], chunks[1][0], chunks[1][1], cos, sin)


def forward_kernel(q_ref, k_ref, v_ref, f_ref, fq_ref, *refs, rows, blocks):
    low_ref, stat_ref = refs[-2:]
    lane = lanes((rows, 128))
    low = lane < 64
    q, fq = q_ref[...], fq_ref[...]
    outs = []
    for x in range(2):
        pick = low if x == 0 else ~low
        qx = jnp.where(pick, q, fq)
        acc = None
        for j in range(blocks):
            sl = pl.ds(j * rows, rows)
            f = f_ref[sl, :]
            kx = jnp.where(pick, k_ref[sl, :], f)
            vx = jnp.where(pick, v_ref[sl, :], f)
            s = nt(qx, kx)
            if j == 0:
                top = jnp.max(s, axis=1, keepdims=True)
            p = jnp.exp2((s - top) * EXP_SCALE).astype(BF)
            a = nn(p, vx)
            acc = a if acc is None else acc + a
        at = 70 if x == 0 else 6
        tot = acc[:, at : at + 1]
        outs.append((acc / tot, jnp.where(lane % 64 == 0, top, tot)))
    (a0, s0), (a1, s1) = outs
    low_ref[...] = jnp.where(low, a0, a1).astype(BF)
    stat_ref[...] = jnp.where(low, s0, s1)


def attend(q, k, v, f, fq, after_this, first, n, into):
    rows, T = q.shape[0], k.shape[0]
    qs = pl.BlockSpec((rows, 128), lambda i: (0, i + first))
    ks = pl.BlockSpec((T, 128), lambda i: (0, i + first))
    cf = pl.BlockSpec((T, 128), lambda i: (0, 0))
    cq = pl.BlockSpec((rows, 128), lambda i: (0, 0))
    anywhere = pl.BlockSpec(memory_space=pl.ANY)
    into = [] if into is None else list(into)
    return pl.pallas_call(
        functools.partial(forward_kernel, rows=rows, blocks=T // rows),
        grid=(n,),
        in_specs=[qs, ks, ks, cf, cq, anywhere] + [anywhere] * len(into),
        out_specs=[qs, qs],
        out_shape=[jax.ShapeDtypeStruct(q.shape, BF), jax.ShapeDtypeStruct(q.shape, F32)],
        input_output_aliases={6 + i: i for i in range(len(into))},
        compiler_params=pltpu.CompilerParams(vmem_limit_bytes=40 * MIB),
        name="attend",
    )(q, k, v, f, fq, after_this, *into)


def backward_kernel(q_ref, k_ref, v_ref, f_ref, fq_ref, stat_ref, mix_ref, gm_ref, cos_ref, sin_ref, *refs, rows, blocks):
    dq_ref, dk_ref, dv_ref, sk_ref, sv_ref = refs[-5:]
    lane = lanes((rows, 128))
    low = lane < 64
    slot = lane % 64
    q = q_ref[...]
    stat = stat_ref[...]
    tot = jnp.where(low, stat[:, 1:2], stat[:, 65:66])
    ga = gm_ref[...] / tot
    prod = ga * mix_ref[...].astype(F32)
    hi, mid, lo = split3(jnp.where(low, stat[:, 64:65], stat[:, 0:1]))
    fq = jnp.where(slot == 3, -hi, jnp.where(slot == 4, -mid, jnp.where(slot == 5, -lo, fq_ref[...].astype(F32)))).astype(BF)
    gab = ga.astype(BF)
    dqs = []
    for x in range(2):
        pick = low if x == 0 else ~low
        qx = jnp.where(pick, q, fq)
        delta = jnp.sum(jnp.where(pick, prod, 0.0), axis=1, keepdims=True)
        h3, m3, l3 = split3(jnp.broadcast_to(delta, (rows, 128)))
        gf = jnp.where(slot == 6, -h3, jnp.where(slot == 7, -m3, jnp.where(slot == 8, -l3, 0.0))).astype(BF)
        gx = jnp.where(pick, gab, gf)
        gxt = gx.T[64 * x : 64 * x + 64]
        qxt = qx.T[64 * x : 64 * x + 64]
        dq = None
        for j in range(blocks):
            sl = pl.ds(j * rows, rows)
            f = f_ref[sl, :]
            kx = jnp.where(pick, k_ref[sl, :], f)
            vx = jnp.where(pick, v_ref[sl, :], f)
            p = jnp.exp2(nt(qx, kx) * EXP_SCALE)
            ds = (p * nt(gx, vx)).astype(BF)
            d = nn(ds, kx)
            dq = d if dq is None else dq + d
            sv_ref[64 * x : 64 * x + 64, sl] = nn(gxt, p.astype(BF))
            sk_ref[64 * x : 64 * x + 64, sl] = nn(qxt, ds)
        dqs.append(dq)
    scale = HEAD_DIM ** (-0.5)

    def unrope(u, sl):
        return (u * cos_ref[sl, :] - swap_halves(u, lane) * sin_ref[sl, :]).astype(BF)

    dq_ref[...] = unrope(jnp.where(low, dqs[0], dqs[1]) * scale, pl.ds(0, rows))
    for j in range(blocks):
        sl = pl.ds(j * rows, rows)
        dv_ref[sl, :] = sv_ref[:, sl].T.astype(BF)
        dk_ref[sl, :] = unrope(sk_ref[:, sl].T * scale, sl)


def attend_back(q, k, v, f, fq, stat, mix, gm, cos, sin, after_this, first, n):
    rows, T = q.shape[0], k.shape[0]
    qs = pl.BlockSpec((rows, 128), lambda i: (0, i + first))
    ks = pl.BlockSpec((T, 128), lambda i: (0, i + first))
    cf = pl.BlockSpec((T, 128), lambda i: (0, 0))
    cq = pl.BlockSpec((rows, 128), lambda i: (0, 0))
    oq = pl.BlockSpec((rows, 128), lambda i: (0, i))
    ok = pl.BlockSpec((T, 128), lambda i: (0, i))
    return pl.pallas_call(
        functools.partial(backward_kernel, rows=rows, blocks=T // rows),
        grid=(n,),
        in_specs=[qs, ks, ks, cf, cq, qs, qs, qs, cf, cf, pl.BlockSpec(memory_space=pl.ANY)],
        out_specs=[oq, ok, ok],
        out_shape=[jax.ShapeDtypeStruct((rows, 128 * n), BF)] + [jax.ShapeDtypeStruct((T, 128 * n), BF)] * 2,
        scratch_shapes=[pltpu.VMEM((128, T), F32), pltpu.VMEM((128, T), F32)],
        compiler_params=pltpu.CompilerParams(vmem_limit_bytes=48 * MIB),
        name="attend_back",
    )(q, k, v, f, fq, stat, mix, gm, cos, sin, after_this)


def mlp_grads_kernel(core_ref, mid_ref, h_ref, mix_ref, branch_ref, gu_ref, ga_ref, give_ref, keep_ref, mid_t, h_t, mix_t, *, F, spots):
    step = pl.program_id(0)

    @pl.when(step == 0)
    def _():
        mid_t[...] = mid_ref[...].T
        h_t[...] = h_ref[...].T
        mix_t[...] = mix_ref[...].T

    def run(out_ref):
        for left, right, mine in ((mid_t, branch_ref, 0), (h_t, gu_ref, 1), (mix_t, ga_ref, 2)):
            for g, n, row, _, wide, col, _ in spots:
                if g == mine:
                    r = nn(left[...], right[:, col : col + wide]).astype(BF)
                    for p in range(F):
                        out_ref[p, row : row + n, :] = r[p * n : (p + 1) * n]

    pl.when(step == 0)(lambda: run(give_ref))
    pl.when(step == 1)(lambda: run(keep_ref))


def mlp_grads(mid, h, mix, branch, gu, ga, core, F, spots, R):
    rows = mid.shape[0]
    half = lambda i, c: (0, 1 - c[0] + i * (2 * c[0] - 1))
    whole = lambda i, c: (0, 0)
    piece = pl.BlockSpec((F, R, 384), lambda i, c: (0, 0, 0))
    out = jax.ShapeDtypeStruct((F, R, 384), BF)
    return pl.pallas_call(
        functools.partial(mlp_grads_kernel, F=F, spots=spots),
        grid_spec=pltpu.PrefetchScalarGridSpec(
            num_scalar_prefetch=1,
            grid=(2,),
            in_specs=[pl.BlockSpec(a.shape, whole) for a in (mid, h, mix)]
            + [pl.BlockSpec((rows, a.shape[1] // 2), half) for a in (branch, gu, ga)],
            out_specs=[piece, piece],
            scratch_shapes=[pltpu.VMEM(a.shape[::-1], BF) for a in (mid, h, mix)],
        ),
        out_shape=[out, out],
        compiler_params=pltpu.CompilerParams(vmem_limit_bytes=40 * MIB),
        name="mlp_grads",
    )(core.reshape(1), mid, h, mix, branch, gu, ga)


def qkv_grads_kernel(core_ref, ht_ref, *refs, F):
    give_ref, keep_ref, ends_ref = refs[-3:]
    parts = refs[:-3]
    count = len(parts) // 3
    width = ht_ref.shape[0]
    n = width // F
    step = pl.program_id(0)
    side = core_ref[0] + (1 - step) * (1 - 2 * core_ref[0])

    def run(out_ref):
        for g in range(3):
            first, *middle, last = parts[g * count : (g + 1) * count]
            depth = first.shape[0]
            end = ends_ref.at[pl.ds(0, depth), :]

            @pl.when(side == 0)
            def _():
                end[...] = first[...]

            @pl.when(side == 1)
            def _():
                end[...] = last[...]

            right = jnp.concatenate([end[...]] + [m[...] for m in middle], axis=1)
            r = nn(ht_ref[:, :depth], right).astype(BF)
            for p in range(F):
                out_ref[p, g * n : (g + 1) * n, :] = r[p * n : (p + 1) * n]

    pl.when(step == 0)(lambda: run(give_ref))
    pl.when(step == 1)(lambda: run(keep_ref))


def qkv_grads(ht, parts, core, F):
    width, T = ht.shape
    half = lambda i, c: (0, 1 - c[0] + i * (2 * c[0] - 1))
    whole = lambda i, c: (0, 0)
    piece = pl.BlockSpec((F, 3 * width // F, width // 2), lambda i, c: (0, 0, 0))
    out = jax.ShapeDtypeStruct((F, 3 * width // F, width // 2), BF)
    return pl.pallas_call(
        functools.partial(qkv_grads_kernel, F=F),
        grid_spec=pltpu.PrefetchScalarGridSpec(
            num_scalar_prefetch=1,
            grid=(2,),
            in_specs=[pl.BlockSpec((width, T), whole)]
            + [pl.BlockSpec((a.shape[0], 128), whole if a.shape[1] == 128 else half) for a in parts],
            out_specs=[piece, piece],
            scratch_shapes=[pltpu.VMEM((T, 128), BF)],
        ),
        out_shape=[out, out],
        compiler_params=pltpu.CompilerParams(vmem_limit_bytes=52 * MIB),
        name="qkv_grads",
    )(core.reshape(1), ht, *parts)


def grad_h_kernel(after_ref, w_ref, *refs, count, own):
    out_ref = refs[-1]
    width = out_ref.shape[1]

    def product(which, offset):
        total = None
        for ref in refs[which * count : (which + 1) * count]:
            r = nt(ref[...], w_ref[:, offset : offset + ref.shape[1]])
            total = r if total is None else total + r
            offset += ref.shape[1]
        return total

    out_ref[...] = (product(1, width) + product(2, 2 * width)).astype(out_ref.dtype)
    if own:

        @pl.when(pl.program_id(0) == 0)
        def _():
            out_ref[...] += product(0, 0)


def grad_h(parts, w, first, blocks, dtype, own, after_this):
    count = len(parts) // 3
    rows, width = parts[0].shape[0], w.shape[0]
    return pl.pallas_call(
        functools.partial(grad_h_kernel, count=count, own=own),
        grid=(blocks,),
        in_specs=[pl.BlockSpec(memory_space=pl.ANY), pl.BlockSpec(w.shape, lambda i: (0, 0))]
        + [pl.BlockSpec(a.shape, lambda i: (0, 0)) for a in parts[:count]]
        + [pl.BlockSpec((rows, a.shape[1]), lambda i: (i + first, 0)) for a in parts[count:]],
        out_specs=pl.BlockSpec((rows, width), lambda i: (i, 0)),
        out_shape=jax.ShapeDtypeStruct((blocks * rows, width), dtype),
        compiler_params=pltpu.CompilerParams(vmem_limit_bytes=40 * MIB),
        name="grad_h",
    )(after_this, w, *parts)


def normalize(fields):
    centred = fields - jnp.mean(fields, axis=-1, keepdims=True)
    variance = jnp.mean(centred * centred, axis=-1, keepdims=True)
    inv_root = lax.rsqrt(variance + norm_eps)
    return centred * inv_root, inv_root


def norm_back(scaled, normed, inv_root):
    return inv_root * (
        scaled
        - jnp.mean(scaled, axis=-1, keepdims=True)
        - normed * jnp.mean(scaled * normed, axis=-1, keepdims=True)
    )


def tables(docs, places):
    lane = jnp.arange(128)
    frequency = rope_base ** (-2.0 * (lane % 32).astype(F32) / HEAD_DIM)
    angles = places.astype(F32)[:, None] * frequency[None, :]
    sign = jnp.where(lane % 64 < 32, -1.0, 1.0)
    slot = lane % 64
    same = (docs[:, None] == slot[None, :]) & (slot < 3)[None, :]
    ones = ((slot >= 3) & (slot < 9))[None, :]
    feats = jnp.where(same | ones, 1.0, 0.0).astype(BF)
    return jnp.cos(angles), jnp.sin(angles) * sign, feats


def core_half(shard, core):
    half = shard.shape[1] // 2
    return lax.dynamic_slice_in_dim(shard, core * half, half, 1)


def gather_steps(piece, pieces, F, C):
    Z = F // 2
    same = piece
    for k in range(Z):
        other = flip_fsdp(same, F, C)
        nxt = ring(same, F, C) if k < Z - 1 else None
        hold = yield same
        if hold is not None:
            other = after(other, hold)
        pieces += [same, other]
        if nxt is not None:
            same = after(nxt, other)


def run_out(steps, hold):
    try:
        steps.send(hold)
        while True:
            next(steps)
    except StopIteration:
        pass


def owners_of(F):
    Z = F // 2
    me = lax.axis_index("fsdp")
    z, xx = me // 2, me % 2
    owners = []
    for k in range(Z):
        base = lax.rem(z - k + Z, Z) * 2
        owners += [base + xx, base + 1 - xx]
    return owners


def both_cores(pieces, F, C):
    chunks = []
    for part in (pieces[:-2], pieces[-2:]):
        own = jnp.concatenate(part[:-1] + [after(part[-1], pieces[-2])], axis=0)
        chunks.append((own, flip_ctx(own, 1, F, C), len(part)))
    return chunks


def body(
    F, C, hidden_in, segment_ids, positions, norm1_gain, qkv_weight, out_weight, norm2_gain, in_weight, down_weight, out_cot
):
    width = hidden_in.shape[-1]
    rows = hidden_in.shape[1]
    inputs = hidden_in.reshape(rows, width)
    docs = segment_ids.reshape(-1)
    places = positions.reshape(-1)
    extra = jnp.zeros((16, width), BF)
    meta = jnp.stack([docs, places // 256, places % 256]).astype(BF)
    extra = lax.dynamic_update_slice(extra, meta, (0, 0))
    core = lax.axis_index("ctx") % 2
    owners = owners_of(F)
    idx = jnp.stack([jnp.asarray(o, jnp.int32) for o in owners] + [core, 1 - core]).astype(jnp.int32)
    n = width // F
    own_gain_one = norm1_gain.astype(F32)[:, None]
    own_gain_two = norm2_gain.astype(F32)[:, None]
    half = (core_half(qkv_weight, core).astype(F32) * own_gain_one).astype(BF)
    scaled_in = (in_weight.astype(F32) * own_gain_two).astype(BF)
    pieces = []
    ring_a = gather_steps(half, pieces, F, C)
    next(ring_a)
    third = [next(ring_a) for _ in range(1)][-1]
    xs = gather_ctx(jnp.concatenate([inputs, extra], axis=0), third, F, C)
    all_meta = jnp.concatenate([x[:, rows : rows + 3, :rows] for x in xs]).astype(jnp.int32)
    all_docs = all_meta[:, 0].reshape(-1)
    all_places = (all_meta[:, 1] * 256 + all_meta[:, 2]).reshape(-1)
    cos, sin, feats = tables(all_docs, all_places)
    for _ in range(F // 2 - 2):
        next(ring_a)
    run_out(ring_a, cos)
    chunks_a = both_cores(pieces, F, C)
    slot = jnp.arange(128) % 64
    query_feats = jnp.where((slot < 3)[None, :] & (docs[:, None] != slot[None, :]), -1e30, 0.0).astype(BF)

    n_down = down_weight.shape[0]
    ring_b = n_down % 16 == 0
    if ring_b:
        wide = core_half(scaled_in, core)
        parts_b = [core_half(out_weight, core)] + [wide[:, j : j + 384] for j in range(0, wide.shape[1], 384)]
        piece_b = jnp.concatenate(parts_b + [core_half(down_weight, core)], axis=0)
        pieces_b = []
        steps_b = gather_steps(after(piece_b, pieces[-1], xs[1]), pieces_b, F, C)
        next(steps_b)
    h_t, query, key, value, w_qkv = project(xs, chunks_a, idx, cos, sin, rows, F)
    pairs = width // 128
    calls = 3
    per = pairs // calls
    mixed = None
    done = query
    for i in range(calls):
        mark = query_feats
        if ring_b:
            mark = steps_b.send(done)
        mixed = attend(query, key, value, feats, query_feats, mark, i * per, per, mixed)
        done = mixed[0]
    mixed_low, stat = mixed
    if ring_b:
        run_out(steps_b, done)
        places = [(0, n, 0, 384, 0, 384)]
        places += [(n * (1 + j), n, 1, wide.shape[1], 384 * j, 384) for j in range(wide.shape[1] // 384)]
        places += [(piece_b.shape[0] - n_down, n_down, 2, 384, 0, 384)]
        shapes = [(width, width), (width, in_weight.shape[1]), (n_down * F, width)]
        w_out, w_in, w_down = unpack(both_cores(pieces_b, F, C), idx, F, places, shapes)
    else:
        w_out, w_in, w_down = [
            lax.all_gather(w, "fsdp", axis=0, tiled=True) for w in (out_weight, scaled_in, down_weight)
        ]

    resid_in = inputs.astype(F32)
    resid = resid_in + nn(mixed_low, w_out)
    normed_two, inv_two = normalize(resid)
    h_two = normed_two.astype(BF)
    ff = w_down.shape[0]
    up_all = nn(h_two, w_in)
    gate, up = up_all[:, :ff], up_all[:, ff:]
    cdf = 0.5 * (1.0 + lax.erf(gate * math.sqrt(0.5)))
    pdf = jnp.exp(-0.5 * gate * gate) * (1.0 / math.sqrt(2.0 * math.pi))
    gelu = gate * cdf
    mid = (gelu * up).astype(BF)
    branch = out_cot.reshape(rows, width)
    grad_mid = nt(branch, w_down)
    grad_u = jnp.concatenate([grad_mid * up * (cdf + gate * pdf), grad_mid * gelu], axis=1).astype(BF)
    grad_h_two = nt(grad_u, w_in)
    grad_resid = branch.astype(F32) + norm_back(grad_h_two, normed_two, inv_two)
    grad_attn = grad_resid.astype(BF)
    grad_mixed = nt(grad_attn, w_out)

    shapes_b = [(ff, width), (width, 2 * ff), (width, width)]
    spots_b, rows_b = pieces_of(shapes_b, F)
    give_b, keep_b = mlp_grads(mid, h_two, mixed_low, branch, grad_u, grad_attn, core, F, spots_b, rows_b)
    sum_b = reduce_steps(give_b, keep_b, spots_b, [(r // F, c) for r, c in shapes_b], {1: (in_weight, own_gain_two)}, F, C)
    back = []
    mark = next(sum_b)
    for first, count in ((0, 1), (1, 2), (3, 2), (5, 1)):
        back.append(
            attend_back(query, key, value, feats, query_feats, stat, mixed_low, grad_mixed, cos, sin, mark, first, count)
        )
        mark = sum_b.send(back[-1][0])
    parts = [b[g] for g in range(3) for b in back]
    give_a, keep_a = qkv_grads(h_t, [after(parts[0], mark)] + parts[1:], core, F)
    sent_b = sum_b.send(give_a)
    spots_a = [
        (0, n, g * n, 128 * i, 128, g * width + c, g * width + d)
        for g in range(3)
        for i, (c, d) in enumerate(((0, 640), (128, 256), (384, 512)))
    ]
    sum_a = reduce_steps(
        after(give_a, sent_b), keep_a, spots_a, [(n, 3 * width)], {0: (qkv_weight, own_gain_one)}, F, C
    )
    next(sum_a)
    far = C // 2
    send_h = grad_h(parts, w_qkv, far, far, BF, False, sent_b)
    acc_a = sum_a.send(send_h)
    near = grad_h(parts, w_qkv, 0, far, F32, True, acc_a)
    stage_a = sum_a.send(near)
    near = near + after(flip_ctx(send_h, 1, F, C), stage_a).astype(F32)
    out = (resid + nn(after(mid, stage_a), w_down)).astype(BF).reshape(hidden_in.shape)
    sum_b.send(stage_a)
    stage_a = sum_a.send((out, near))
    g_down, g_in, g_out, g_gain_two = finish(sum_b, stage_a)
    stage_a = sum_a.send(g_in)
    grad_h_one = after(reduce_ctx(near.reshape(far, rows, width), ctx_bits(C)[:-1], F, C), stage_a)
    normed_one, inv_one = normalize(after(inputs, stage_a).astype(F32))
    in_grad = (grad_resid + norm_back(grad_h_one, normed_one, inv_one)).reshape(hidden_in.shape)
    g_qkv, g_gain_one = finish(sum_a, in_grad)
    g_gain_one, g_gain_two = g_gain_one.reshape(-1), g_gain_two.reshape(-1)
    return (out, in_grad, g_gain_one, g_qkv, g_out, g_gain_two, g_in, g_down)


def solution(mesh):
    F, C = mesh.shape["fsdp"], mesh.shape["ctx"]
    tokens = P("fsdp", "ctx", None)
    ids = P("fsdp", "ctx")
    vec = P("fsdp")
    mat = P("fsdp", None)
    return jax.shard_map(
        functools.partial(body, F, C),
        mesh=mesh,
        in_specs=(tokens, ids, ids, vec, mat, mat, vec, mat, mat, tokens),
        out_specs=(tokens, tokens, vec, mat, mat, vec, mat, mat),
        check_vma=False,
    )
```

```python
import functools
import math

import jax
import jax.numpy as jnp
from jax import lax
from jax.experimental import pallas as pl
from jax.experimental.pallas import tpu as pltpu
from jax.sharding import PartitionSpec as P

HEAD_DIM = 64
rope_base = 160000.0
norm_eps = 1e-05
BF = jnp.bfloat16
F32 = jnp.float32
AXES = ("fsdp", "ctx")
EXP_SCALE = HEAD_DIM ** (-0.5) * math.log2(math.e)
MIB = 2**20


def nt(a, b):
    return lax.dot_general(a, b, (((1,), (1,)), ((), ())), preferred_element_type=F32)


def nn(a, b):
    return lax.dot_general(a, b, (((1,), (0,)), ((), ())), preferred_element_type=F32)


def tn(a, b):
    return lax.dot_general(a, b, (((0,), (0,)), ((), ())), preferred_element_type=F32)


def lanes(shape):
    return lax.broadcasted_iota(jnp.int32, shape, 1)


def split3(v):
    hi = v.astype(BF).astype(F32)
    rest = v - hi
    mid = rest.astype(BF).astype(F32)
    low = (rest - mid).astype(BF).astype(F32)
    return hi, mid, low


def swap_halves(u, lane):
    width = u.shape[1]
    return jnp.where((lane % 64) < 32, pltpu.roll(u, width - 32, 1), pltpu.roll(u, 32, 1))


def permute(x, fn, F, C):
    return lax.ppermute(x, AXES, [(i, fn(i)) for i in range(F * C)])


def after(x, *others):
    return lax.optimization_barrier((x,) + others)[0]


def beside(x, hold):
    return x if hold is None else after(x, *(hold if isinstance(hold, tuple) else (hold,)))


def flip_ctx(x, bit, F, C):
    return permute(x, lambda i: (i // C) * C + ((i % C) ^ bit), F, C)


def flip_fsdp(x, F, C):
    return permute(x, lambda i: (((i // C) ^ 1) * C) + i % C, F, C)


def ring(x, F, C):
    return permute(x, lambda i: (i + 2 * C) % (F * C), F, C)


def ctx_bits(C):
    bits = []
    b = C // 2
    while b:
        bits.append(b)
        b //= 2
    return bits


def gather_ctx(x, hold, F, C):
    have = x[None]
    bits = ctx_bits(C)
    for b in bits[:-1]:
        have = jnp.concatenate([have, after(flip_ctx(have, b, F, C), hold)], axis=0)
    return have, flip_ctx(have, bits[-1], F, C)


def reduce_ctx(parts, bits, F, C):
    for b in reversed(bits):
        half = parts.shape[0] // 2
        got = flip_ctx(parts[half:].astype(BF), b, F, C)
        parts = parts[:half] + got.astype(F32)
    return parts[0]


def reduce_steps(give, keep, spots, shapes, scaled, F, C):
    core = lax.axis_index("ctx") % 2
    me = lax.axis_index("fsdp")
    Z = F // 2
    z, xx = me // 2, me % 2
    hold = yield give
    got = beside(flip_ctx(give, 1, F, C), hold)
    ring_order = [lax.rem(z - 1 - s + Z, Z) * 2 for s in range(Z)]
    order = [d + side for d in ring_order for side in (xx, 1 - xx)]
    acc = add_sorted(keep, got, order)
    hold = yield acc[1]
    total = None
    for s in range(Z):
        give = acc[2 * s + 1]
        got = beside(flip_fsdp(give if s == 0 else after(give, send), F, C), hold)
        mine = acc[2 * s].astype(F32) + got.astype(F32)
        total = mine if total is None else mine + arrived.astype(F32)
        if s < Z - 1:
            send = total.astype(BF)
            hold = yield send
            arrived = ring(send, F, C)
    for b in ctx_bits(C)[:-1]:
        send = total.astype(BF)
        hold = yield send
        total = total + beside(flip_ctx(send, b, F, C), hold).astype(F32)
    send = total.astype(BF)
    hold = yield send
    other = beside(flip_ctx(send, 1, F, C), hold)
    yield spread(total, other, core, spots, shapes, scaled)


def finish(steps, hold=None):
    last = next(steps) if hold is None else steps.send(hold)
    for last in steps:
        pass
    return last


def place_pieces(idx_ref, chunks, outs, places, sems, F):
    made = []
    at = 0
    for own_ref, got_ref, count in chunks:
        piece = own_ref.shape[0] // count
        for j in range(count):
            for side, src in ((0, own_ref), (1, got_ref)):
                for row, n, o, half, col, wide in places:
                    r = pl.multiple_of(idx_ref[at + j] * n, n)
                    c = pl.multiple_of(idx_ref[F + side] * half + col, 128)
                    made.append(
                        pltpu.make_async_copy(
                            src.at[pl.ds(j * piece + row, n), :],
                            outs[o].at[pl.ds(r, n), pl.ds(c, wide)],
                            sems.at[len(made)],
                        )
                    )
        at += count
    return made


def unpack_kernel(idx_ref, a_ref, b_ref, c_ref, d_ref, *refs, F, places, counts):
    chunks = [(a_ref, b_ref, counts[0]), (c_ref, d_ref, counts[1])]
    made = place_pieces(idx_ref, chunks, refs[:-1], places, refs[-1], F)
    for c in made:
        c.start()
    for c in made:
        c.wait()


def unpack(chunks, idx, F, places, shapes):
    anywhere = pl.BlockSpec(memory_space=pl.ANY)
    return pl.pallas_call(
        functools.partial(unpack_kernel, F=F, places=places, counts=[c[2] for c in chunks]),
        in_specs=[pl.BlockSpec(memory_space=pltpu.SMEM)] + [anywhere] * 4,
        out_specs=[pl.BlockSpec(memory_space=pltpu.VMEM)] * len(shapes),
        out_shape=[jax.ShapeDtypeStruct(s, BF) for s in shapes],
        scratch_shapes=[pltpu.SemaphoreType.DMA((2 * F * len(places),))],
        compiler_params=pltpu.CompilerParams(vmem_limit_bytes=32 * MIB),
        name="unpack",
    )(idx, chunks[0][0], chunks[0][1], chunks[1][0], chunks[1][1])


def pieces_of(grads, F):
    spots = []
    row = 0
    for g, (rows, cols) in enumerate(grads):
        n = rows // F
        for j in range(0, cols // 2, 384):
            spots.append((g, n, row, 0, 384, j, cols // 2 + j))
            row += n
    return spots, row


def add_sorted_kernel(idx_ref, keep_ref, got_ref, *outs):
    for j, out in enumerate(outs):
        i = idx_ref[j]
        out[...] = (keep_ref[i].astype(F32) + got_ref[i].astype(F32)).astype(BF)


def add_sorted(keep, got, order):
    vmem = pl.BlockSpec(memory_space=pltpu.VMEM)
    return pl.pallas_call(
        add_sorted_kernel,
        in_specs=[pl.BlockSpec(memory_space=pltpu.SMEM), vmem, vmem],
        out_specs=[vmem] * len(order),
        out_shape=[jax.ShapeDtypeStruct(keep.shape[1:], BF)] * len(order),
        compiler_params=pltpu.CompilerParams(vmem_limit_bytes=32 * MIB),
        name="add_sorted",
    )(jnp.stack(order).astype(jnp.int32), keep, got)


def spread_kernel(core_ref, own_ref, other_ref, *refs, spots, scaled):
    weights = [(refs[2 * i], refs[2 * i + 1]) for i in range(len(scaled))]
    outs = refs[2 * len(scaled) :]

    def write(side):
        for g, n, row, at, wide, *cols in spots:
            c, d = cols[side], cols[1 - side]
            outs[g][:, c : c + wide] = own_ref[row : row + n, at : at + wide]
            outs[g][:, d : d + wide] = other_ref[row : row + n, at : at + wide].astype(F32)

    pl.when(core_ref[0] == 0)(lambda: write(0))
    pl.when(core_ref[0] == 1)(lambda: write(1))
    for (w_ref, gain_ref), g, sum_ref in zip(weights, scaled, outs[len(outs) - len(scaled) :]):
        v = outs[g][...]
        sums = jnp.sum(v * w_ref[...].astype(F32), axis=1, keepdims=True)
        sum_ref[...] = jnp.broadcast_to(sums, (v.shape[0], 128)).T[:1]
        outs[g][...] = v * gain_ref[...]


def spread(own, other, core, spots, shapes, scaled):
    vmem = pl.BlockSpec(memory_space=pltpu.VMEM)
    more = [a for pair in scaled.values() for a in pair]
    outs = [jax.ShapeDtypeStruct(s, F32) for s in shapes]
    outs += [jax.ShapeDtypeStruct((1, shapes[g][0]), F32) for g in scaled]
    return pl.pallas_call(
        functools.partial(spread_kernel, spots=spots, scaled=list(scaled)),
        in_specs=[pl.BlockSpec(memory_space=pltpu.SMEM), vmem, vmem] + [vmem] * len(more),
        out_specs=[vmem] * len(outs),
        out_shape=outs,
        name="spread",
    )(core.reshape(1), own, other, *more)


def project_kernel(idx_ref, x_ref, y_ref, a_ref, b_ref, c_ref, d_ref, cos_ref, sin_ref, h_ref, q_ref, k_ref, v_ref, w_ref, sems, *, F, n, counts):
    width, rows = h_ref.shape
    half = w_ref.shape[1] // 2
    chunks = [(a_ref, b_ref, counts[0]), (c_ref, d_ref, counts[1])]
    made = place_pieces(idx_ref, chunks, [w_ref], [(0, n, 0, half, 0, half)], sems, F)

    @pl.when(pl.program_id(0) == 0)
    def _():
        for c in made:
            c.start()

    x = jnp.where(pl.program_id(0) < pl.num_programs(0) // 2, x_ref[0, :rows, :], y_ref[0, :rows, :]).astype(F32)
    centred = x - jnp.mean(x, axis=1, keepdims=True)
    var = jnp.mean(centred * centred, axis=1, keepdims=True)
    h = (centred * lax.rsqrt(var + norm_eps)).astype(BF)
    h_ref[...] = h.T

    @pl.when(pl.program_id(0) == 0)
    def _():
        for c in made:
            c.wait()

    cos, sin = cos_ref[...], sin_ref[...]
    lane = lanes((rows, 128))

    def rope_into(ref, offset):
        for j in range(0, width, 256):
            u = nn(h, w_ref[:, offset + j : offset + j + 256])
            for i in (0, 128):
                t = u[:, i : i + 128]
                ref[:, j + i : j + i + 128] = (t * cos + swap_halves(t, lane) * sin).astype(BF)

    rope_into(k_ref, width)
    for j in range(0, width, 256):
        v_ref[:, j : j + 256] = nn(h, w_ref[:, 2 * width + j : 2 * width + j + 256]).astype(BF)

    @pl.when(pl.program_id(0) == 0)
    def _():
        rope_into(q_ref, 0)


def project(xs, chunks, idx, cos, sin, rows, F):
    near, far = xs
    C, width = 2 * near.shape[0], near.shape[2]
    blk = pl.BlockSpec((rows, width), lambda i: (i, 0))
    tab = pl.BlockSpec((rows, 128), lambda i: (i, 0))
    whole = lambda i: (0, 0)
    out = jax.ShapeDtypeStruct((C * rows, width), BF)
    return pl.pallas_call(
        functools.partial(project_kernel, F=F, n=width // F, counts=[c[2] for c in chunks]),
        grid=(C,),
        in_specs=[
            pl.BlockSpec(memory_space=pltpu.SMEM),
            pl.BlockSpec((1,) + near.shape[1:], lambda i: (jnp.minimum(i, C // 2 - 1), 0, 0)),
            pl.BlockSpec((1,) + near.shape[1:], lambda i: (jnp.maximum(i - C // 2, 0), 0, 0)),
        ]
        + [pl.BlockSpec(memory_space=pl.ANY)] * 4
        + [tab, tab],
        out_specs=[
            pl.BlockSpec((width, rows), lambda i: (0, i)),
            pl.BlockSpec((rows, width), whole),
            blk,
            blk,
            pl.BlockSpec((width, 3 * width), whole),
        ],
        out_shape=[jax.ShapeDtypeStruct((width, C * rows), BF), jax.ShapeDtypeStruct((rows, width), BF), out, out, jax.ShapeDtypeStruct((width, 3 * width), BF)],
        scratch_shapes=[pltpu.SemaphoreType.DMA((2 * F,))],
        compiler_params=pltpu.CompilerParams(vmem_limit_bytes=60 * MIB),
        name="project",
    )(idx, near, far, chunks[0][0], chunks[0][1], chunks[1][0], chunks[1][1], cos, sin)


def forward_kernel(q_ref, k_ref, v_ref, f_ref, fq_ref, *refs, rows, blocks):
    low_ref, stat_ref = refs[-2:]
    lane = lanes((rows, 128))
    low = lane < 64
    q, fq = q_ref[...], fq_ref[...]
    outs = []
    for x in range(2):
        pick = low if x == 0 else ~low
        qx = jnp.where(pick, q, fq)
        acc = None
        for j in range(blocks):
            sl = pl.ds(j * rows, rows)
            f = f_ref[sl, :]
            kx = jnp.where(pick, k_ref[sl, :], f)
            vx = jnp.where(pick, v_ref[sl, :], f)
            s = nt(qx, kx)
            if j == 0:
                top = jnp.max(s, axis=1, keepdims=True)
            p = jnp.exp2((s - top) * EXP_SCALE).astype(BF)
            a = nn(p, vx)
            acc = a if acc is None else acc + a
        at = 70 if x == 0 else 6
        tot = acc[:, at : at + 1]
        outs.append((acc / tot, jnp.where(lane % 64 == 0, top, tot)))
    (a0, s0), (a1, s1) = outs
    low_ref[...] = jnp.where(low, a0, a1).astype(BF)
    stat_ref[...] = jnp.where(low, s0, s1)


def attend(q, k, v, f, fq, after_this, first, n, into):
    rows, T = q.shape[0], k.shape[0]
    qs = pl.BlockSpec((rows, 128), lambda i: (0, i + first))
    ks = pl.BlockSpec((T, 128), lambda i: (0, i + first))
    cf = pl.BlockSpec((T, 128), lambda i: (0, 0))
    cq = pl.BlockSpec((rows, 128), lambda i: (0, 0))
    anywhere = pl.BlockSpec(memory_space=pl.ANY)
    into = [] if into is None else list(into)
    return pl.pallas_call(
        functools.partial(forward_kernel, rows=rows, blocks=T // rows),
        grid=(n,),
        in_specs=[qs, ks, ks, cf, cq, anywhere] + [anywhere] * len(into),
        out_specs=[qs, qs],
        out_shape=[jax.ShapeDtypeStruct(q.shape, BF), jax.ShapeDtypeStruct(q.shape, F32)],
        input_output_aliases={6 + i: i for i in range(len(into))},
        compiler_params=pltpu.CompilerParams(vmem_limit_bytes=40 * MIB),
        name="attend",
    )(q, k, v, f, fq, after_this, *into)


def backward_kernel(q_ref, k_ref, v_ref, f_ref, fq_ref, stat_ref, mix_ref, gm_ref, cos_ref, sin_ref, *refs, rows, blocks):
    dq_ref, dk_ref, dv_ref, sk_ref, sv_ref = refs[-5:]
    lane = lanes((rows, 128))
    low = lane < 64
    slot = lane % 64
    q = q_ref[...]
    stat = stat_ref[...]
    tot = jnp.where(low, stat[:, 1:2], stat[:, 65:66])
    ga = gm_ref[...] / tot
    prod = ga * mix_ref[...].astype(F32)
    hi, mid, lo = split3(jnp.where(low, stat[:, 64:65], stat[:, 0:1]))
    fq = jnp.where(slot == 3, -hi, jnp.where(slot == 4, -mid, jnp.where(slot == 5, -lo, fq_ref[...].astype(F32)))).astype(BF)
    gab = ga.astype(BF)
    dqs = []
    for x in range(2):
        pick = low if x == 0 else ~low
        qx = jnp.where(pick, q, fq)
        delta = jnp.sum(jnp.where(pick, prod, 0.0), axis=1, keepdims=True)
        h3, m3, l3 = split3(jnp.broadcast_to(delta, (rows, 128)))
        gf = jnp.where(slot == 6, -h3, jnp.where(slot == 7, -m3, jnp.where(slot == 8, -l3, 0.0))).astype(BF)
        gx = jnp.where(pick, gab, gf)
        gxt = gx.T[64 * x : 64 * x + 64]
        qxt = qx.T[64 * x : 64 * x + 64]
        dq = None
        for j in range(blocks):
            sl = pl.ds(j * rows, rows)
            f = f_ref[sl, :]
            kx = jnp.where(pick, k_ref[sl, :], f)
            vx = jnp.where(pick, v_ref[sl, :], f)
            p = jnp.exp2(nt(qx, kx) * EXP_SCALE)
            ds = (p * nt(gx, vx)).astype(BF)
            d = nn(ds, kx)
            dq = d if dq is None else dq + d
            sv_ref[64 * x : 64 * x + 64, sl] = nn(gxt, p.astype(BF))
            sk_ref[64 * x : 64 * x + 64, sl] = nn(qxt, ds)
        dqs.append(dq)
    scale = HEAD_DIM ** (-0.5)

    def unrope(u, sl):
        return (u * cos_ref[sl, :] - swap_halves(u, lane) * sin_ref[sl, :]).astype(BF)

    dq_ref[...] = unrope(jnp.where(low, dqs[0], dqs[1]) * scale, pl.ds(0, rows))
    for j in range(blocks):
        sl = pl.ds(j * rows, rows)
        dv_ref[sl, :] = sv_ref[:, sl].T.astype(BF)
        dk_ref[sl, :] = unrope(sk_ref[:, sl].T * scale, sl)


def attend_back(q, k, v, f, fq, stat, mix, gm, cos, sin, after_this, first, n):
    rows, T = q.shape[0], k.shape[0]
    qs = pl.BlockSpec((rows, 128), lambda i: (0, i + first))
    ks = pl.BlockSpec((T, 128), lambda i: (0, i + first))
    cf = pl.BlockSpec((T, 128), lambda i: (0, 0))
    cq = pl.BlockSpec((rows, 128), lambda i: (0, 0))
    oq = pl.BlockSpec((rows, 128), lambda i: (0, i))
    ok = pl.BlockSpec((T, 128), lambda i: (0, i))
    return pl.pallas_call(
        functools.partial(backward_kernel, rows=rows, blocks=T // rows),
        grid=(n,),
        in_specs=[qs, ks, ks, cf, cq, qs, qs, qs, cf, cf, pl.BlockSpec(memory_space=pl.ANY)],
        out_specs=[oq, ok, ok],
        out_shape=[jax.ShapeDtypeStruct((rows, 128 * n), BF)] + [jax.ShapeDtypeStruct((T, 128 * n), BF)] * 2,
        scratch_shapes=[pltpu.VMEM((128, T), F32), pltpu.VMEM((128, T), F32)],
        compiler_params=pltpu.CompilerParams(vmem_limit_bytes=48 * MIB),
        name="attend_back",
    )(q, k, v, f, fq, stat, mix, gm, cos, sin, after_this)


def mlp_grads_kernel(core_ref, mid_ref, h_ref, mix_ref, branch_ref, gu_ref, ga_ref, give_ref, keep_ref, mid_t, h_t, mix_t, *, F, spots):
    step = pl.program_id(0)

    @pl.when(step == 0)
    def _():
        mid_t[...] = mid_ref[...].T
        h_t[...] = h_ref[...].T
        mix_t[...] = mix_ref[...].T

    def run(out_ref):
        for left, right, mine in ((mid_t, branch_ref, 0), (h_t, gu_ref, 1), (mix_t, ga_ref, 2)):
            for g, n, row, _, wide, col, _ in spots:
                if g == mine:
                    r = nn(left[...], right[:, col : col + wide]).astype(BF)
                    for p in range(F):
                        out_ref[p, row : row + n, :] = r[p * n : (p + 1) * n]

    pl.when(step == 0)(lambda: run(give_ref))
    pl.when(step == 1)(lambda: run(keep_ref))


def mlp_grads(mid, h, mix, branch, gu, ga, core, F, spots, R):
    rows = mid.shape[0]
    half = lambda i, c: (0, 1 - c[0] + i * (2 * c[0] - 1))
    whole = lambda i, c: (0, 0)
    piece = pl.BlockSpec((F, R, 384), lambda i, c: (0, 0, 0))
    out = jax.ShapeDtypeStruct((F, R, 384), BF)
    return pl.pallas_call(
        functools.partial(mlp_grads_kernel, F=F, spots=spots),
        grid_spec=pltpu.PrefetchScalarGridSpec(
            num_scalar_prefetch=1,
            grid=(2,),
            in_specs=[pl.BlockSpec(a.shape, whole) for a in (mid, h, mix)]
            + [pl.BlockSpec((rows, a.shape[1] // 2), half) for a in (branch, gu, ga)],
            out_specs=[piece, piece],
            scratch_shapes=[pltpu.VMEM(a.shape[::-1], BF) for a in (mid, h, mix)],
        ),
        out_shape=[out, out],
        compiler_params=pltpu.CompilerParams(vmem_limit_bytes=40 * MIB),
        name="mlp_grads",
    )(core.reshape(1), mid, h, mix, branch, gu, ga)


def qkv_grads_kernel(core_ref, ht_ref, *refs, F):
    give_ref, keep_ref = refs[-2:]
    parts = refs[:-2]
    count = len(parts) // 3
    width = ht_ref.shape[0]
    n = width // F

    def run(out_ref):
        for g in range(3):
            right = jnp.concatenate([parts[g * count + i][...] for i in range(count)], axis=1)
            r = nn(ht_ref[:, : right.shape[0]], right).astype(BF)
            for p in range(F):
                out_ref[p, g * n : (g + 1) * n, :] = r[p * n : (p + 1) * n]

    step = pl.program_id(0)
    pl.when(step == 0)(lambda: run(give_ref))
    pl.when(step == 1)(lambda: run(keep_ref))


def qkv_grads(ht, parts, core, F):
    width, T = ht.shape
    half = lambda i, c: (0, 1 - c[0] + i * (2 * c[0] - 1))
    piece = pl.BlockSpec((F, 3 * width // F, width // 2), lambda i, c: (0, 0, 0))
    out = jax.ShapeDtypeStruct((F, 3 * width // F, width // 2), BF)
    return pl.pallas_call(
        functools.partial(qkv_grads_kernel, F=F),
        grid_spec=pltpu.PrefetchScalarGridSpec(
            num_scalar_prefetch=1,
            grid=(2,),
            in_specs=[pl.BlockSpec((width, T), lambda i, c: (0, 0))] + [pl.BlockSpec((a.shape[0], 128), half) for a in parts],
            out_specs=[piece, piece],
        ),
        out_shape=[out, out],
        compiler_params=pltpu.CompilerParams(vmem_limit_bytes=52 * MIB),
        name="qkv_grads",
    )(core.reshape(1), ht, *parts)


def grad_h_kernel(after_ref, w_ref, *refs, count, own):
    out_ref = refs[-1]
    width = out_ref.shape[1]
    wide = width // count

    def product(which, offset):
        total = None
        for i in range(count):
            c = offset + i * wide
            r = nt(refs[which * count + i][...], w_ref[:, c : c + wide])
            total = r if total is None else total + r
        return total

    out_ref[...] = (product(1, width) + product(2, 2 * width)).astype(out_ref.dtype)
    if own:

        @pl.when(pl.program_id(0) == 0)
        def _():
            out_ref[...] += product(0, 0)


def grad_h(parts, w, first, blocks, dtype, own, after_this):
    count = len(parts) // 3
    rows, width = parts[0].shape[0], w.shape[0]
    return pl.pallas_call(
        functools.partial(grad_h_kernel, count=count, own=own),
        grid=(blocks,),
        in_specs=[pl.BlockSpec(memory_space=pl.ANY), pl.BlockSpec(w.shape, lambda i: (0, 0))]
        + [pl.BlockSpec(a.shape, lambda i: (0, 0)) for a in parts[:count]]
        + [pl.BlockSpec((rows, a.shape[1]), lambda i: (i + first, 0)) for a in parts[count:]],
        out_specs=pl.BlockSpec((rows, width), lambda i: (i, 0)),
        out_shape=jax.ShapeDtypeStruct((blocks * rows, width), dtype),
        compiler_params=pltpu.CompilerParams(vmem_limit_bytes=40 * MIB),
        name="grad_h",
    )(after_this, w, *parts)


def normalize(fields):
    centred = fields - jnp.mean(fields, axis=-1, keepdims=True)
    variance = jnp.mean(centred * centred, axis=-1, keepdims=True)
    inv_root = lax.rsqrt(variance + norm_eps)
    return centred * inv_root, inv_root


def norm_back(scaled, normed, inv_root):
    return inv_root * (
        scaled
        - jnp.mean(scaled, axis=-1, keepdims=True)
        - normed * jnp.mean(scaled * normed, axis=-1, keepdims=True)
    )


def tables(docs, places):
    lane = jnp.arange(128)
    frequency = rope_base ** (-2.0 * (lane % 32).astype(F32) / HEAD_DIM)
    angles = places.astype(F32)[:, None] * frequency[None, :]
    sign = jnp.where(lane % 64 < 32, -1.0, 1.0)
    slot = lane % 64
    same = (docs[:, None] == slot[None, :]) & (slot < 3)[None, :]
    ones = ((slot >= 3) & (slot < 9))[None, :]
    feats = jnp.where(same | ones, 1.0, 0.0).astype(BF)
    return jnp.cos(angles), jnp.sin(angles) * sign, feats


def core_half(shard, core):
    half = shard.shape[1] // 2
    return lax.dynamic_slice_in_dim(shard, core * half, half, 1)


def gather_steps(piece, pieces, F, C):
    Z = F // 2
    same = piece
    for k in range(Z):
        other = flip_fsdp(same, F, C)
        nxt = ring(same, F, C) if k < Z - 1 else None
        hold = yield same
        if hold is not None:
            other = after(other, hold)
        pieces += [same, other]
        if nxt is not None:
            same = after(nxt, other)


def run_out(steps, hold):
    try:
        steps.send(hold)
        while True:
            next(steps)
    except StopIteration:
        pass


def owners_of(F):
    Z = F // 2
    me = lax.axis_index("fsdp")
    z, xx = me // 2, me % 2
    owners = []
    for k in range(Z):
        base = lax.rem(z - k + Z, Z) * 2
        owners += [base + xx, base + 1 - xx]
    return owners


def both_cores(pieces, F, C):
    chunks = []
    for part in (pieces[:-2], pieces[-2:]):
        own = jnp.concatenate(part[:-1] + [after(part[-1], pieces[-2])], axis=0)
        chunks.append((own, flip_ctx(own, 1, F, C), len(part)))
    return chunks


def body(
    F, C, hidden_in, segment_ids, positions, norm1_gain, qkv_weight, out_weight, norm2_gain, in_weight, down_weight, out_cot
):
    width = hidden_in.shape[-1]
    rows = hidden_in.shape[1]
    inputs = hidden_in.reshape(rows, width)
    docs = segment_ids.reshape(-1)
    places = positions.reshape(-1)
    extra = jnp.zeros((16, width), BF)
    meta = jnp.stack([docs, places // 256, places % 256]).astype(BF)
    extra = lax.dynamic_update_slice(extra, meta, (0, 0))
    core = lax.axis_index("ctx") % 2
    owners = owners_of(F)
    idx = jnp.stack([jnp.asarray(o, jnp.int32) for o in owners] + [core, 1 - core]).astype(jnp.int32)
    n = width // F
    own_gain_one = norm1_gain.astype(F32)[:, None]
    own_gain_two = norm2_gain.astype(F32)[:, None]
    half = (core_half(qkv_weight, core).astype(F32) * own_gain_one).astype(BF)
    scaled_in = (in_weight.astype(F32) * own_gain_two).astype(BF)
    pieces = []
    ring_a = gather_steps(half, pieces, F, C)
    next(ring_a)
    next(ring_a)
    third = next(ring_a)
    xs = gather_ctx(jnp.concatenate([inputs, extra], axis=0), third, F, C)
    all_meta = jnp.concatenate([x[:, rows : rows + 3, :rows] for x in xs]).astype(jnp.int32)
    all_docs = all_meta[:, 0].reshape(-1)
    all_places = (all_meta[:, 1] * 256 + all_meta[:, 2]).reshape(-1)
    cos, sin, feats = tables(all_docs, all_places)
    for _ in range(F // 2 - 3):
        next(ring_a)
    run_out(ring_a, cos)
    chunks_a = both_cores(pieces, F, C)
    slot = jnp.arange(128) % 64
    query_feats = jnp.where((slot < 3)[None, :] & (docs[:, None] != slot[None, :]), -1e30, 0.0).astype(BF)

    n_down = down_weight.shape[0]
    ring_b = n_down % 16 == 0
    if ring_b:
        wide = core_half(scaled_in, core)
        parts_b = [core_half(out_weight, core)] + [wide[:, j : j + 384] for j in range(0, wide.shape[1], 384)]
        piece_b = jnp.concatenate(parts_b + [core_half(down_weight, core)], axis=0)
        pieces_b = []
        steps_b = gather_steps(after(piece_b, pieces[-1], xs[1]), pieces_b, F, C)
        next(steps_b)
    h_t, query, key, value, w_qkv = project(xs, chunks_a, idx, cos, sin, rows, F)
    pairs = width // 128
    calls = 3
    per = pairs // calls
    mixed = None
    done = query
    for i in range(calls):
        mark = query_feats
        if ring_b:
            mark = steps_b.send(done)
        mixed = attend(query, key, value, feats, query_feats, mark, i * per, per, mixed)
        done = mixed[0]
    mixed_low, stat = mixed
    if ring_b:
        run_out(steps_b, done)
        places = [(0, n, 0, 384, 0, 384)]
        places += [(n * (1 + j), n, 1, wide.shape[1], 384 * j, 384) for j in range(wide.shape[1] // 384)]
        places += [(piece_b.shape[0] - n_down, n_down, 2, 384, 0, 384)]
        shapes = [(width, width), (width, in_weight.shape[1]), (n_down * F, width)]
        w_out, w_in, w_down = unpack(both_cores(pieces_b, F, C), idx, F, places, shapes)
    else:
        w_out, w_in, w_down = [
            lax.all_gather(w, "fsdp", axis=0, tiled=True) for w in (out_weight, scaled_in, down_weight)
        ]

    resid_in = inputs.astype(F32)
    resid = resid_in + nn(mixed_low, w_out)
    normed_two, inv_two = normalize(resid)
    h_two = normed_two.astype(BF)
    ff = w_down.shape[0]
    up_all = nn(h_two, w_in)
    gate, up = up_all[:, :ff], up_all[:, ff:]
    cdf = 0.5 * (1.0 + lax.erf(gate * math.sqrt(0.5)))
    pdf = jnp.exp(-0.5 * gate * gate) * (1.0 / math.sqrt(2.0 * math.pi))
    gelu = gate * cdf
    mid = (gelu * up).astype(BF)
    branch = out_cot.reshape(rows, width)
    grad_mid = nt(branch, w_down)
    grad_u = jnp.concatenate([grad_mid * up * (cdf + gate * pdf), grad_mid * gelu], axis=1).astype(BF)
    grad_h_two = nt(grad_u, w_in)
    grad_resid = branch.astype(F32) + norm_back(grad_h_two, normed_two, inv_two)
    grad_attn = grad_resid.astype(BF)
    grad_mixed = nt(grad_attn, w_out)

    shapes_b = [(ff, width), (width, 2 * ff), (width, width)]
    spots_b, rows_b = pieces_of(shapes_b, F)
    give_b, keep_b = mlp_grads(mid, h_two, mixed_low, branch, grad_u, grad_attn, core, F, spots_b, rows_b)
    sum_b = reduce_steps(give_b, keep_b, spots_b, [(r // F, c) for r, c in shapes_b], {1: (in_weight, own_gain_two)}, F, C)
    back = []
    mark = next(sum_b)
    for i in range(calls):
        back.append(
            attend_back(query, key, value, feats, query_feats, stat, mixed_low, grad_mixed, cos, sin, mark, i * per, per)
        )
        mark = sum_b.send(back[-1][0])
    parts = [b[g] for g in range(3) for b in back]
    give_a, keep_a = qkv_grads(h_t, [after(parts[0], mark)] + parts[1:], core, F)
    sent_b = sum_b.send(give_a)
    spots_a = [
        (0, n, g * n, 128 * i, 128, g * width + 256 * i, g * width + 256 * i + 128) for g in range(3) for i in range(calls)
    ]
    sum_a = reduce_steps(after(give_a, sent_b), keep_a, spots_a, [(n, 3 * width)], {0: (qkv_weight, own_gain_one)}, F, C)
    next(sum_a)
    far = C // 2
    send_h = grad_h(parts, w_qkv, far, far, BF, False, sent_b)
    acc_a = sum_a.send(send_h)
    near = grad_h(parts, w_qkv, 0, far, F32, True, acc_a)
    stage_b = sum_b.send(near)
    stage_a = sum_a.send(stage_b)
    got_h = after(flip_ctx(send_h, 1, F, C), stage_a).astype(F32)
    near = near + got_h
    out = (resid + nn(after(mid, stage_a), w_down)).astype(BF).reshape(hidden_in.shape)
    stage_a = sum_a.send((out, near))
    stage_b = sum_b.send(stage_a)
    stage_a = sum_a.send(stage_b)
    g_down, g_in, g_out, g_gain_two = finish(sum_b, stage_a)
    grad_h_one = after(reduce_ctx(near.reshape(far, rows, width), ctx_bits(C)[:-1], F, C), stage_a)
    normed_one, inv_one = normalize(after(inputs, stage_a).astype(F32))
    in_grad = (grad_resid + norm_back(grad_h_one, normed_one, inv_one)).reshape(hidden_in.shape)
    g_qkv, g_gain_one = finish(sum_a, (in_grad, g_in))
    g_gain_one, g_gain_two = g_gain_one.reshape(-1), g_gain_two.reshape(-1)
    return (out, in_grad, g_gain_one, g_qkv, g_out, g_gain_two, g_in, g_down)


def solution(mesh):
    F, C = mesh.shape["fsdp"], mesh.shape["ctx"]
    tokens = P("fsdp", "ctx", None)
    ids = P("fsdp", "ctx")
    vec = P("fsdp")
    mat = P("fsdp", None)
    return jax.shard_map(
        functools.partial(body, F, C),
        mesh=mesh,
        in_specs=(tokens, ids, ids, vec, mat, mat, vec, mat, mat, tokens),
        out_specs=(tokens, tokens, vec, mat, mat, vec, mat, mat),
        check_vma=False,
    )
```

```python
import functools
import math

import jax
import jax.numpy as jnp
from jax import lax
from jax.experimental import pallas as pl
from jax.experimental.pallas import tpu as pltpu
from jax.sharding import PartitionSpec as P

HEAD_DIM = 64
rope_base = 160000.0
norm_eps = 1e-05
BF = jnp.bfloat16
F32 = jnp.float32
AXES = ("fsdp", "ctx")
EXP_SCALE = HEAD_DIM ** (-0.5) * math.log2(math.e)
MIB = 2**20


def nt(a, b):
    return lax.dot_general(a, b, (((1,), (1,)), ((), ())), preferred_element_type=F32)


def nn(a, b):
    return lax.dot_general(a, b, (((1,), (0,)), ((), ())), preferred_element_type=F32)


def tn(a, b):
    return lax.dot_general(a, b, (((0,), (0,)), ((), ())), preferred_element_type=F32)


def lanes(shape):
    return lax.broadcasted_iota(jnp.int32, shape, 1)


def split3(v):
    hi = v.astype(BF).astype(F32)
    rest = v - hi
    mid = rest.astype(BF).astype(F32)
    low = (rest - mid).astype(BF).astype(F32)
    return hi, mid, low


def swap_halves(u, lane):
    width = u.shape[1]
    return jnp.where((lane % 64) < 32, pltpu.roll(u, width - 32, 1), pltpu.roll(u, 32, 1))


def permute(x, fn, F, C):
    return lax.ppermute(x, AXES, [(i, fn(i)) for i in range(F * C)])


def after(x, *others):
    return lax.optimization_barrier((x,) + others)[0]


def beside(x, hold):
    return x if hold is None else after(x, *(hold if isinstance(hold, tuple) else (hold,)))


def flip_ctx(x, bit, F, C):
    return permute(x, lambda i: (i // C) * C + ((i % C) ^ bit), F, C)


def flip_fsdp(x, F, C):
    return permute(x, lambda i: (((i // C) ^ 1) * C) + i % C, F, C)


def ring(x, F, C):
    return permute(x, lambda i: (i + 2 * C) % (F * C), F, C)


def ctx_bits(C):
    bits = []
    b = C // 2
    while b:
        bits.append(b)
        b //= 2
    return bits


def gather_ctx(x, hold, F, C):
    have = x[None]
    bits = ctx_bits(C)
    for b in bits[:-1]:
        have = jnp.concatenate([have, after(flip_ctx(have, b, F, C), hold)], axis=0)
    return have, flip_ctx(have, bits[-1], F, C)


def reduce_ctx(parts, bits, F, C):
    for b in reversed(bits):
        half = parts.shape[0] // 2
        got = flip_ctx(parts[half:].astype(BF), b, F, C)
        parts = parts[:half] + got.astype(F32)
    return parts[0]


def reduce_steps(give, keep, spots, shapes, scaled, F, C):
    core = lax.axis_index("ctx") % 2
    me = lax.axis_index("fsdp")
    Z = F // 2
    z, xx = me // 2, me % 2
    hold = yield give
    got = beside(flip_ctx(give, 1, F, C), hold)
    ring_order = [lax.rem(z - 1 - s + Z, Z) * 2 for s in range(Z)]
    order = [d + side for d in ring_order for side in (xx, 1 - xx)]
    acc = add_sorted(keep, got, order)
    hold = yield acc[1]
    total = None
    for s in range(Z):
        give = acc[2 * s + 1]
        got = beside(flip_fsdp(give if s == 0 else after(give, send), F, C), hold)
        mine = acc[2 * s].astype(F32) + got.astype(F32)
        total = mine if total is None else mine + arrived.astype(F32)
        if s < Z - 1:
            send = total.astype(BF)
            hold = yield send
            arrived = ring(send, F, C)
    for b in ctx_bits(C)[:-1]:
        send = total.astype(BF)
        hold = yield send
        total = total + beside(flip_ctx(send, b, F, C), hold).astype(F32)
    send = total.astype(BF)
    hold = yield send
    other = beside(flip_ctx(send, 1, F, C), hold)
    yield spread(total, other, core, spots, shapes, scaled)


def finish(steps, hold=None):
    last = next(steps) if hold is None else steps.send(hold)
    for last in steps:
        pass
    return last


def place_pieces(idx_ref, chunks, outs, places, sems, F):
    made = []
    at = 0
    for own_ref, got_ref, count in chunks:
        piece = own_ref.shape[0] // count
        for j in range(count):
            for side, src in ((0, own_ref), (1, got_ref)):
                for row, n, o, half, col, wide in places:
                    r = pl.multiple_of(idx_ref[at + j] * n, n)
                    c = pl.multiple_of(idx_ref[F + side] * half + col, 128)
                    made.append(
                        pltpu.make_async_copy(
                            src.at[pl.ds(j * piece + row, n), :],
                            outs[o].at[pl.ds(r, n), pl.ds(c, wide)],
                            sems.at[len(made)],
                        )
                    )
        at += count
    return made


def unpack_kernel(idx_ref, a_ref, b_ref, c_ref, d_ref, *refs, F, places, counts):
    chunks = [(a_ref, b_ref, counts[0]), (c_ref, d_ref, counts[1])]
    made = place_pieces(idx_ref, chunks, refs[:-1], places, refs[-1], F)
    for c in made:
        c.start()
    for c in made:
        c.wait()


def unpack(chunks, idx, F, places, shapes):
    anywhere = pl.BlockSpec(memory_space=pl.ANY)
    return pl.pallas_call(
        functools.partial(unpack_kernel, F=F, places=places, counts=[c[2] for c in chunks]),
        in_specs=[pl.BlockSpec(memory_space=pltpu.SMEM)] + [anywhere] * 4,
        out_specs=[pl.BlockSpec(memory_space=pltpu.VMEM)] * len(shapes),
        out_shape=[jax.ShapeDtypeStruct(s, BF) for s in shapes],
        scratch_shapes=[pltpu.SemaphoreType.DMA((2 * F * len(places),))],
        compiler_params=pltpu.CompilerParams(vmem_limit_bytes=32 * MIB),
        name="unpack",
    )(idx, chunks[0][0], chunks[0][1], chunks[1][0], chunks[1][1])


def pieces_of(grads, F):
    spots = []
    row = 0
    for g, (rows, cols) in enumerate(grads):
        n = rows // F
        for j in range(0, cols // 2, 384):
            spots.append((g, n, row, 0, 384, j, cols // 2 + j))
            row += n
    return spots, row


def add_sorted_kernel(idx_ref, keep_ref, got_ref, *outs):
    for j, out in enumerate(outs):
        i = idx_ref[j]
        out[...] = (keep_ref[i].astype(F32) + got_ref[i].astype(F32)).astype(BF)


def add_sorted(keep, got, order):
    vmem = pl.BlockSpec(memory_space=pltpu.VMEM)
    return pl.pallas_call(
        add_sorted_kernel,
        in_specs=[pl.BlockSpec(memory_space=pltpu.SMEM), vmem, vmem],
        out_specs=[vmem] * len(order),
        out_shape=[jax.ShapeDtypeStruct(keep.shape[1:], BF)] * len(order),
        compiler_params=pltpu.CompilerParams(vmem_limit_bytes=32 * MIB),
        name="add_sorted",
    )(jnp.stack(order).astype(jnp.int32), keep, got)


def spread_kernel(core_ref, own_ref, other_ref, *refs, spots, scaled):
    weights = [(refs[2 * i], refs[2 * i + 1]) for i in range(len(scaled))]
    outs = refs[2 * len(scaled) :]

    def write(side):
        for g, n, row, at, wide, *cols in spots:
            c, d = cols[side], cols[1 - side]
            outs[g][:, c : c + wide] = own_ref[row : row + n, at : at + wide]
            outs[g][:, d : d + wide] = other_ref[row : row + n, at : at + wide].astype(F32)

    pl.when(core_ref[0] == 0)(lambda: write(0))
    pl.when(core_ref[0] == 1)(lambda: write(1))
    for (w_ref, gain_ref), g, sum_ref in zip(weights, scaled, outs[len(outs) - len(scaled) :]):
        v = outs[g][...]
        sums = jnp.sum(v * w_ref[...].astype(F32), axis=1, keepdims=True)
        sum_ref[...] = jnp.broadcast_to(sums, (v.shape[0], 128)).T[:1]
        outs[g][...] = v * gain_ref[...]


def spread(own, other, core, spots, shapes, scaled):
    vmem = pl.BlockSpec(memory_space=pltpu.VMEM)
    more = [a for pair in scaled.values() for a in pair]
    outs = [jax.ShapeDtypeStruct(s, F32) for s in shapes]
    outs += [jax.ShapeDtypeStruct((1, shapes[g][0]), F32) for g in scaled]
    return pl.pallas_call(
        functools.partial(spread_kernel, spots=spots, scaled=list(scaled)),
        in_specs=[pl.BlockSpec(memory_space=pltpu.SMEM), vmem, vmem] + [vmem] * len(more),
        out_specs=[vmem] * len(outs),
        out_shape=outs,
        name="spread",
    )(core.reshape(1), own, other, *more)


def project_kernel(idx_ref, x_ref, y_ref, a_ref, b_ref, c_ref, d_ref, cos_ref, sin_ref, h_ref, q_ref, k_ref, v_ref, w_ref, sems, *, F, n, counts):
    width, rows = h_ref.shape
    half = w_ref.shape[1] // 2
    chunks = [(a_ref, b_ref, counts[0]), (c_ref, d_ref, counts[1])]
    made = place_pieces(idx_ref, chunks, [w_ref], [(0, n, 0, half, 0, half)], sems, F)

    @pl.when(pl.program_id(0) == 0)
    def _():
        for c in made:
            c.start()

    x = jnp.where(pl.program_id(0) < pl.num_programs(0) // 2, x_ref[0, :rows, :], y_ref[0, :rows, :]).astype(F32)
    centred = x - jnp.mean(x, axis=1, keepdims=True)
    var = jnp.mean(centred * centred, axis=1, keepdims=True)
    h = (centred * lax.rsqrt(var + norm_eps)).astype(BF)
    h_ref[...] = h.T

    @pl.when(pl.program_id(0) == 0)
    def _():
        for c in made:
            c.wait()

    cos, sin = cos_ref[...], sin_ref[...]
    lane = lanes((rows, 128))

    def rope_into(ref, offset):
        for j in range(0, width, 256):
            u = nn(h, w_ref[:, offset + j : offset + j + 256])
            for i in (0, 128):
                t = u[:, i : i + 128]
                ref[:, j + i : j + i + 128] = (t * cos + swap_halves(t, lane) * sin).astype(BF)

    rope_into(k_ref, width)
    for j in range(0, width, 256):
        v_ref[:, j : j + 256] = nn(h, w_ref[:, 2 * width + j : 2 * width + j + 256]).astype(BF)

    @pl.when(pl.program_id(0) == 0)
    def _():
        rope_into(q_ref, 0)


def project(xs, chunks, idx, cos, sin, rows, F):
    near, far = xs
    C, width = 2 * near.shape[0], near.shape[2]
    blk = pl.BlockSpec((rows, width), lambda i: (i, 0))
    tab = pl.BlockSpec((rows, 128), lambda i: (i, 0))
    whole = lambda i: (0, 0)
    out = jax.ShapeDtypeStruct((C * rows, width), BF)
    return pl.pallas_call(
        functools.partial(project_kernel, F=F, n=width // F, counts=[c[2] for c in chunks]),
        grid=(C,),
        in_specs=[
            pl.BlockSpec(memory_space=pltpu.SMEM),
            pl.BlockSpec((1,) + near.shape[1:], lambda i: (jnp.minimum(i, C // 2 - 1), 0, 0)),
            pl.BlockSpec((1,) + near.shape[1:], lambda i: (jnp.maximum(i - C // 2, 0), 0, 0)),
        ]
        + [pl.BlockSpec(memory_space=pl.ANY)] * 4
        + [tab, tab],
        out_specs=[
            pl.BlockSpec((width, rows), lambda i: (0, i)),
            pl.BlockSpec((rows, width), whole),
            blk,
            blk,
            pl.BlockSpec((width, 3 * width), whole),
        ],
        out_shape=[jax.ShapeDtypeStruct((width, C * rows), BF), jax.ShapeDtypeStruct((rows, width), BF), out, out, jax.ShapeDtypeStruct((width, 3 * width), BF)],
        scratch_shapes=[pltpu.SemaphoreType.DMA((2 * F,))],
        compiler_params=pltpu.CompilerParams(vmem_limit_bytes=60 * MIB),
        name="project",
    )(idx, near, far, chunks[0][0], chunks[0][1], chunks[1][0], chunks[1][1], cos, sin)


def forward_kernel(q_ref, k_ref, v_ref, f_ref, fq_ref, *refs, rows, blocks):
    low_ref, stat_ref = refs[-2:]
    lane = lanes((rows, 128))
    low = lane < 64
    q, fq = q_ref[...], fq_ref[...]
    outs = []
    for x in range(2):
        pick = low if x == 0 else ~low
        qx = jnp.where(pick, q, fq)
        acc = None
        for j in range(blocks):
            sl = pl.ds(j * rows, rows)
            f = f_ref[sl, :]
            kx = jnp.where(pick, k_ref[sl, :], f)
            vx = jnp.where(pick, v_ref[sl, :], f)
            s = nt(qx, kx)
            if j == 0:
                top = jnp.max(s, axis=1, keepdims=True)
            p = jnp.exp2((s - top) * EXP_SCALE).astype(BF)
            a = nn(p, vx)
            acc = a if acc is None else acc + a
        at = 70 if x == 0 else 6
        tot = acc[:, at : at + 1]
        outs.append((acc / tot, jnp.where(lane % 64 == 0, top, tot)))
    (a0, s0), (a1, s1) = outs
    low_ref[...] = jnp.where(low, a0, a1).astype(BF)
    stat_ref[...] = jnp.where(low, s0, s1)


def attend(q, k, v, f, fq, after_this, first, n, into):
    rows, T = q.shape[0], k.shape[0]
    qs = pl.BlockSpec((rows, 128), lambda i: (0, i + first))
    ks = pl.BlockSpec((T, 128), lambda i: (0, i + first))
    cf = pl.BlockSpec((T, 128), lambda i: (0, 0))
    cq = pl.BlockSpec((rows, 128), lambda i: (0, 0))
    anywhere = pl.BlockSpec(memory_space=pl.ANY)
    into = [] if into is None else list(into)
    return pl.pallas_call(
        functools.partial(forward_kernel, rows=rows, blocks=T // rows),
        grid=(n,),
        in_specs=[qs, ks, ks, cf, cq, anywhere] + [anywhere] * len(into),
        out_specs=[qs, qs],
        out_shape=[jax.ShapeDtypeStruct(q.shape, BF), jax.ShapeDtypeStruct(q.shape, F32)],
        input_output_aliases={6 + i: i for i in range(len(into))},
        compiler_params=pltpu.CompilerParams(vmem_limit_bytes=40 * MIB),
        name="attend",
    )(q, k, v, f, fq, after_this, *into)


def backward_kernel(q_ref, k_ref, v_ref, f_ref, fq_ref, stat_ref, mix_ref, gm_ref, cos_ref, sin_ref, *refs, rows, blocks):
    dq_ref, dk_ref, dv_ref, sk_ref, sv_ref = refs[-5:]
    lane = lanes((rows, 128))
    low = lane < 64
    slot = lane % 64
    q = q_ref[...]
    stat = stat_ref[...]
    tot = jnp.where(low, stat[:, 1:2], stat[:, 65:66])
    ga = gm_ref[...] / tot
    prod = ga * mix_ref[...].astype(F32)
    hi, mid, lo = split3(jnp.where(low, stat[:, 64:65], stat[:, 0:1]))
    fq = jnp.where(slot == 3, -hi, jnp.where(slot == 4, -mid, jnp.where(slot == 5, -lo, fq_ref[...].astype(F32)))).astype(BF)
    gab = ga.astype(BF)
    dqs = []
    for x in range(2):
        pick = low if x == 0 else ~low
        qx = jnp.where(pick, q, fq)
        delta = jnp.sum(jnp.where(pick, prod, 0.0), axis=1, keepdims=True)
        h3, m3, l3 = split3(jnp.broadcast_to(delta, (rows, 128)))
        gf = jnp.where(slot == 6, -h3, jnp.where(slot == 7, -m3, jnp.where(slot == 8, -l3, 0.0))).astype(BF)
        gx = jnp.where(pick, gab, gf)
        gxt = gx.T[64 * x : 64 * x + 64]
        qxt = qx.T[64 * x : 64 * x + 64]
        dq = None
        for j in range(blocks):
            sl = pl.ds(j * rows, rows)
            f = f_ref[sl, :]
            kx = jnp.where(pick, k_ref[sl, :], f)
            vx = jnp.where(pick, v_ref[sl, :], f)
            p = jnp.exp2(nt(qx, kx) * EXP_SCALE)
            ds = (p * nt(gx, vx)).astype(BF)
            d = nn(ds, kx)
            dq = d if dq is None else dq + d
            sv_ref[64 * x : 64 * x + 64, sl] = nn(gxt, p.astype(BF))
            sk_ref[64 * x : 64 * x + 64, sl] = nn(qxt, ds)
        dqs.append(dq)
    scale = HEAD_DIM ** (-0.5)

    def unrope(u, sl):
        return (u * cos_ref[sl, :] - swap_halves(u, lane) * sin_ref[sl, :]).astype(BF)

    dq_ref[...] = unrope(jnp.where(low, dqs[0], dqs[1]) * scale, pl.ds(0, rows))
    for j in range(blocks):
        sl = pl.ds(j * rows, rows)
        dv_ref[sl, :] = sv_ref[:, sl].T.astype(BF)
        dk_ref[sl, :] = unrope(sk_ref[:, sl].T * scale, sl)


def attend_back(q, k, v, f, fq, stat, mix, gm, cos, sin, after_this, first, n):
    rows, T = q.shape[0], k.shape[0]
    qs = pl.BlockSpec((rows, 128), lambda i: (0, i + first))
    ks = pl.BlockSpec((T, 128), lambda i: (0, i + first))
    cf = pl.BlockSpec((T, 128), lambda i: (0, 0))
    cq = pl.BlockSpec((rows, 128), lambda i: (0, 0))
    oq = pl.BlockSpec((rows, 128), lambda i: (0, i))
    ok = pl.BlockSpec((T, 128), lambda i: (0, i))
    return pl.pallas_call(
        functools.partial(backward_kernel, rows=rows, blocks=T // rows),
        grid=(n,),
        in_specs=[qs, ks, ks, cf, cq, qs, qs, qs, cf, cf, pl.BlockSpec(memory_space=pl.ANY)],
        out_specs=[oq, ok, ok],
        out_shape=[jax.ShapeDtypeStruct((rows, 128 * n), BF)] + [jax.ShapeDtypeStruct((T, 128 * n), BF)] * 2,
        scratch_shapes=[pltpu.VMEM((128, T), F32), pltpu.VMEM((128, T), F32)],
        compiler_params=pltpu.CompilerParams(vmem_limit_bytes=48 * MIB),
        name="attend_back",
    )(q, k, v, f, fq, stat, mix, gm, cos, sin, after_this)


def mlp_grads_kernel(core_ref, mid_ref, h_ref, mix_ref, branch_ref, gu_ref, ga_ref, give_ref, keep_ref, mid_t, h_t, mix_t, *, F, spots):
    step = pl.program_id(0)

    @pl.when(step == 0)
    def _():
        mid_t[...] = mid_ref[...].T
        h_t[...] = h_ref[...].T
        mix_t[...] = mix_ref[...].T

    def run(out_ref):
        for left, right, mine in ((mid_t, branch_ref, 0), (h_t, gu_ref, 1), (mix_t, ga_ref, 2)):
            for g, n, row, _, wide, col, _ in spots:
                if g == mine:
                    r = nn(left[...], right[:, col : col + wide]).astype(BF)
                    for p in range(F):
                        out_ref[p, row : row + n, :] = r[p * n : (p + 1) * n]

    pl.when(step == 0)(lambda: run(give_ref))
    pl.when(step == 1)(lambda: run(keep_ref))


def mlp_grads(mid, h, mix, branch, gu, ga, core, F, spots, R):
    rows = mid.shape[0]
    half = lambda i, c: (0, 1 - c[0] + i * (2 * c[0] - 1))
    whole = lambda i, c: (0, 0)
    piece = pl.BlockSpec((F, R, 384), lambda i, c: (0, 0, 0))
    out = jax.ShapeDtypeStruct((F, R, 384), BF)
    return pl.pallas_call(
        functools.partial(mlp_grads_kernel, F=F, spots=spots),
        grid_spec=pltpu.PrefetchScalarGridSpec(
            num_scalar_prefetch=1,
            grid=(2,),
            in_specs=[pl.BlockSpec(a.shape, whole) for a in (mid, h, mix)]
            + [pl.BlockSpec((rows, a.shape[1] // 2), half) for a in (branch, gu, ga)],
            out_specs=[piece, piece],
            scratch_shapes=[pltpu.VMEM(a.shape[::-1], BF) for a in (mid, h, mix)],
        ),
        out_shape=[out, out],
        compiler_params=pltpu.CompilerParams(vmem_limit_bytes=40 * MIB),
        name="mlp_grads",
    )(core.reshape(1), mid, h, mix, branch, gu, ga)


def qkv_grads_kernel(core_ref, ht_ref, *refs, F):
    give_ref, keep_ref = refs[-2:]
    parts = refs[:-2]
    count = len(parts) // 3
    width = ht_ref.shape[0]
    n = width // F

    def run(out_ref):
        for g in range(3):
            right = jnp.concatenate([parts[g * count + i][...] for i in range(count)], axis=1)
            r = nn(ht_ref[:, : right.shape[0]], right).astype(BF)
            for p in range(F):
                out_ref[p, g * n : (g + 1) * n, :] = r[p * n : (p + 1) * n]

    step = pl.program_id(0)
    pl.when(step == 0)(lambda: run(give_ref))
    pl.when(step == 1)(lambda: run(keep_ref))


def qkv_grads(ht, parts, core, F):
    width, T = ht.shape
    half = lambda i, c: (0, 1 - c[0] + i * (2 * c[0] - 1))
    piece = pl.BlockSpec((F, 3 * width // F, width // 2), lambda i, c: (0, 0, 0))
    out = jax.ShapeDtypeStruct((F, 3 * width // F, width // 2), BF)
    return pl.pallas_call(
        functools.partial(qkv_grads_kernel, F=F),
        grid_spec=pltpu.PrefetchScalarGridSpec(
            num_scalar_prefetch=1,
            grid=(2,),
            in_specs=[pl.BlockSpec((width, T), lambda i, c: (0, 0))] + [pl.BlockSpec((a.shape[0], 128), half) for a in parts],
            out_specs=[piece, piece],
        ),
        out_shape=[out, out],
        compiler_params=pltpu.CompilerParams(vmem_limit_bytes=52 * MIB),
        name="qkv_grads",
    )(core.reshape(1), ht, *parts)


def grad_h_kernel(after_ref, w_ref, *refs, count, own):
    out_ref = refs[-1]
    width = out_ref.shape[1]
    wide = width // count

    def product(which, offset):
        total = None
        for i in range(count):
            c = offset + i * wide
            r = nt(refs[which * count + i][...], w_ref[:, c : c + wide])
            total = r if total is None else total + r
        return total

    out_ref[...] = (product(1, width) + product(2, 2 * width)).astype(out_ref.dtype)
    if own:

        @pl.when(pl.program_id(0) == 0)
        def _():
            out_ref[...] += product(0, 0)


def grad_h(parts, w, first, blocks, dtype, own, after_this):
    count = len(parts) // 3
    rows, width = parts[0].shape[0], w.shape[0]
    return pl.pallas_call(
        functools.partial(grad_h_kernel, count=count, own=own),
        grid=(blocks,),
        in_specs=[pl.BlockSpec(memory_space=pl.ANY), pl.BlockSpec(w.shape, lambda i: (0, 0))]
        + [pl.BlockSpec(a.shape, lambda i: (0, 0)) for a in parts[:count]]
        + [pl.BlockSpec((rows, a.shape[1]), lambda i: (i + first, 0)) for a in parts[count:]],
        out_specs=pl.BlockSpec((rows, width), lambda i: (i, 0)),
        out_shape=jax.ShapeDtypeStruct((blocks * rows, width), dtype),
        compiler_params=pltpu.CompilerParams(vmem_limit_bytes=40 * MIB),
        name="grad_h",
    )(after_this, w, *parts)


def normalize(fields):
    centred = fields - jnp.mean(fields, axis=-1, keepdims=True)
    variance = jnp.mean(centred * centred, axis=-1, keepdims=True)
    inv_root = lax.rsqrt(variance + norm_eps)
    return centred * inv_root, inv_root


def norm_back(scaled, normed, inv_root):
    return inv_root * (
        scaled
        - jnp.mean(scaled, axis=-1, keepdims=True)
        - normed * jnp.mean(scaled * normed, axis=-1, keepdims=True)
    )


def tables(docs, places):
    lane = jnp.arange(128)
    frequency = rope_base ** (-2.0 * (lane % 32).astype(F32) / HEAD_DIM)
    angles = places.astype(F32)[:, None] * frequency[None, :]
    sign = jnp.where(lane % 64 < 32, -1.0, 1.0)
    slot = lane % 64
    same = (docs[:, None] == slot[None, :]) & (slot < 3)[None, :]
    ones = ((slot >= 3) & (slot < 9))[None, :]
    feats = jnp.where(same | ones, 1.0, 0.0).astype(BF)
    return jnp.cos(angles), jnp.sin(angles) * sign, feats


def core_half(shard, core):
    half = shard.shape[1] // 2
    return lax.dynamic_slice_in_dim(shard, core * half, half, 1)


def gather_steps(piece, pieces, F, C):
    Z = F // 2
    same = piece
    for k in range(Z):
        other = flip_fsdp(same, F, C)
        nxt = ring(same, F, C) if k < Z - 1 else None
        hold = yield same
        if hold is not None:
            other = after(other, hold)
        pieces += [same, other]
        if nxt is not None:
            same = after(nxt, other)


def run_out(steps, hold):
    try:
        steps.send(hold)
        while True:
            next(steps)
    except StopIteration:
        pass


def owners_of(F):
    Z = F // 2
    me = lax.axis_index("fsdp")
    z, xx = me // 2, me % 2
    owners = []
    for k in range(Z):
        base = lax.rem(z - k + Z, Z) * 2
        owners += [base + xx, base + 1 - xx]
    return owners


def both_cores(pieces, F, C):
    chunks = []
    for part in (pieces[:-2], pieces[-2:]):
        own = jnp.concatenate(part[:-1] + [after(part[-1], pieces[-2])], axis=0)
        chunks.append((own, flip_ctx(own, 1, F, C), len(part)))
    return chunks


def body(
    F, C, hidden_in, segment_ids, positions, norm1_gain, qkv_weight, out_weight, norm2_gain, in_weight, down_weight, out_cot
):
    width = hidden_in.shape[-1]
    rows = hidden_in.shape[1]
    inputs = hidden_in.reshape(rows, width)
    docs = segment_ids.reshape(-1)
    places = positions.reshape(-1)
    extra = jnp.zeros((16, width), BF)
    meta = jnp.stack([docs, places // 256, places % 256]).astype(BF)
    extra = lax.dynamic_update_slice(extra, meta, (0, 0))
    core = lax.axis_index("ctx") % 2
    owners = owners_of(F)
    idx = jnp.stack([jnp.asarray(o, jnp.int32) for o in owners] + [core, 1 - core]).astype(jnp.int32)
    n = width // F
    own_gain_one = norm1_gain.astype(F32)[:, None]
    own_gain_two = norm2_gain.astype(F32)[:, None]
    half = (core_half(qkv_weight, core).astype(F32) * own_gain_one).astype(BF)
    scaled_in = (in_weight.astype(F32) * own_gain_two).astype(BF)
    pieces = []
    ring_a = gather_steps(half, pieces, F, C)
    next(ring_a)
    next(ring_a)
    third = next(ring_a)
    xs = gather_ctx(jnp.concatenate([inputs, extra], axis=0), third, F, C)
    all_meta = jnp.concatenate([x[:, rows : rows + 3, :rows] for x in xs]).astype(jnp.int32)
    all_docs = all_meta[:, 0].reshape(-1)
    all_places = (all_meta[:, 1] * 256 + all_meta[:, 2]).reshape(-1)
    cos, sin, feats = tables(all_docs, all_places)
    for _ in range(F // 2 - 3):
        next(ring_a)
    run_out(ring_a, cos)
    chunks_a = both_cores(pieces, F, C)
    slot = jnp.arange(128) % 64
    query_feats = jnp.where((slot < 3)[None, :] & (docs[:, None] != slot[None, :]), -1e30, 0.0).astype(BF)

    n_down = down_weight.shape[0]
    ring_b = n_down % 16 == 0
    if ring_b:
        wide = core_half(scaled_in, core)
        parts_b = [core_half(out_weight, core)] + [wide[:, j : j + 384] for j in range(0, wide.shape[1], 384)]
        piece_b = jnp.concatenate(parts_b + [core_half(down_weight, core)], axis=0)
        pieces_b = []
        steps_b = gather_steps(after(piece_b, pieces[-2]), pieces_b, F, C)
        next(steps_b)
        idx_a = after(idx, steps_b.send(chunks_a[1][0]))
    else:
        idx_a = idx
    h_t, query, key, value, w_qkv = project(xs, chunks_a, idx_a, cos, sin, rows, F)
    pairs = width // 128
    calls = 3
    per = pairs // calls
    mixed = None
    done = query
    for i in range(calls):
        if not ring_b:
            mark = query_feats
        elif i < 2:
            mark = steps_b.send(done)
        mixed = attend(query, key, value, feats, query_feats, mark, i * per, per, mixed)
        done = mixed[0]
    mixed_low, stat = mixed
    if ring_b:
        run_out(steps_b, done)
        places = [(0, n, 0, 384, 0, 384)]
        places += [(n * (1 + j), n, 1, wide.shape[1], 384 * j, 384) for j in range(wide.shape[1] // 384)]
        places += [(piece_b.shape[0] - n_down, n_down, 2, 384, 0, 384)]
        shapes = [(width, width), (width, in_weight.shape[1]), (n_down * F, width)]
        w_out, w_in, w_down = unpack(both_cores(pieces_b, F, C), idx, F, places, shapes)
    else:
        w_out, w_in, w_down = [
            lax.all_gather(w, "fsdp", axis=0, tiled=True) for w in (out_weight, scaled_in, down_weight)
        ]

    resid_in = inputs.astype(F32)
    resid = resid_in + nn(mixed_low, w_out)
    normed_two, inv_two = normalize(resid)
    h_two = normed_two.astype(BF)
    ff = w_down.shape[0]
    up_all = nn(h_two, w_in)
    gate, up = up_all[:, :ff], up_all[:, ff:]
    cdf = 0.5 * (1.0 + lax.erf(gate * math.sqrt(0.5)))
    pdf = jnp.exp(-0.5 * gate * gate) * (1.0 / math.sqrt(2.0 * math.pi))
    gelu = gate * cdf
    mid = (gelu * up).astype(BF)
    branch = out_cot.reshape(rows, width)
    grad_mid = nt(branch, w_down)
    grad_u = jnp.concatenate([grad_mid * up * (cdf + gate * pdf), grad_mid * gelu], axis=1).astype(BF)
    grad_h_two = nt(grad_u, w_in)
    grad_resid = branch.astype(F32) + norm_back(grad_h_two, normed_two, inv_two)
    grad_attn = grad_resid.astype(BF)
    grad_mixed = nt(grad_attn, w_out)

    shapes_b = [(ff, width), (width, 2 * ff), (width, width)]
    spots_b, rows_b = pieces_of(shapes_b, F)
    give_b, keep_b = mlp_grads(mid, h_two, mixed_low, branch, grad_u, grad_attn, core, F, spots_b, rows_b)
    sum_b = reduce_steps(give_b, keep_b, spots_b, [(r // F, c) for r, c in shapes_b], {1: (in_weight, own_gain_two)}, F, C)
    back = []
    mark = next(sum_b)
    for i in range(calls):
        back.append(
            attend_back(query, key, value, feats, query_feats, stat, mixed_low, grad_mixed, cos, sin, mark, i * per, per)
        )
        mark = sum_b.send(back[-1][0])
    parts = [b[g] for g in range(3) for b in back]
    give_a, keep_a = qkv_grads(h_t, [after(parts[0], mark)] + parts[1:], core, F)
    sent_b = sum_b.send(give_a)
    spots_a = [
        (0, n, g * n, 128 * i, 128, g * width + 256 * i, g * width + 256 * i + 128) for g in range(3) for i in range(calls)
    ]
    sum_a = reduce_steps(after(give_a, sent_b), keep_a, spots_a, [(n, 3 * width)], {0: (qkv_weight, own_gain_one)}, F, C)
    next(sum_a)
    far = C // 2
    send_h = grad_h(parts, w_qkv, far, far, BF, False, sent_b)
    acc_a = sum_a.send(send_h)
    near = grad_h(parts, w_qkv, 0, far, F32, True, acc_a)
    stage_b = sum_b.send(near)
    stage_a = sum_a.send(stage_b)
    got_h = after(flip_ctx(send_h, 1, F, C), stage_a).astype(F32)
    near = near + got_h
    out = (resid + nn(after(mid, stage_a), w_down)).astype(BF).reshape(hidden_in.shape)
    stage_a = sum_a.send((out, near))
    stage_b = sum_b.send(stage_a)
    stage_a = sum_a.send(stage_b)
    g_down, g_in, g_out, g_gain_two = finish(sum_b, stage_a)
    grad_h_one = after(reduce_ctx(near.reshape(far, rows, width), ctx_bits(C)[:-1], F, C), stage_a)
    normed_one, inv_one = normalize(after(inputs, stage_a).astype(F32))
    in_grad = (grad_resid + norm_back(grad_h_one, normed_one, inv_one)).reshape(hidden_in.shape)
    g_qkv, g_gain_one = finish(sum_a, (in_grad, g_in))
    g_gain_one, g_gain_two = g_gain_one.reshape(-1), g_gain_two.reshape(-1)
    return (out, in_grad, g_gain_one, g_qkv, g_out, g_gain_two, g_in, g_down)


def solution(mesh):
    F, C = mesh.shape["fsdp"], mesh.shape["ctx"]
    tokens = P("fsdp", "ctx", None)
    ids = P("fsdp", "ctx")
    vec = P("fsdp")
    mat = P("fsdp", None)
    return jax.shard_map(
        functools.partial(body, F, C),
        mesh=mesh,
        in_specs=(tokens, ids, ids, vec, mat, mat, vec, mat, mat, tokens),
        out_specs=(tokens, tokens, vec, mat, mat, vec, mat, mat),
        check_vma=False,
    )
```
